32 devices in a mesh: blk: 8 (over z, y), grp: 4 (over x, core).
Axes of the slice: x: 2, y: 2, z: 4, core: 2. Of those that a mesh axis runs over, the one named last changes fastest.
Arguments:
- acts: bfloat16 [1, 128, 256, 4096], P(None, 'blk', 'grp'), may hold values from -6 to 6
- out_grads: bfloat16 [1, 128, 256, 4096], P(None, 'blk', 'grp'), may hold values from -6 to 6
- proj_in: bfloat16 [1, 4096, 64], replicated, may hold values from -0.09375 to 0.09375
- proj_out: bfloat16 [1, 4096, 64], replicated, may hold values from -0.09375 to 0.09375
- lengths: int32 [128], P('blk'), may hold values from 1 to 256
- queries: bfloat16 [512, 4096], P('blk'), may hold values from -0.09375 to 0.09375
Outputs:
- scores: float32 [128, 512], P(('blk', 'grp'))
The draws below stay inside these ranges and needn't reach their ends.
All inputs are finite; a program needn't handle non-finite values.
Results may differ from the reference program's by a relative error of at most 0.0049.
Values may be sent and summed in bfloat16 or wider, within the bound.
No kernel may reach another device: no remote copies, remote signals or barrier semaphores. Data moves between devices by JAX's collectives and lax.ppermute only.
A program may use at most 128 MiB of HBM per device.

```python
import jax
import jax.numpy as jnp
from jax import lax

D = 4096
PR = 64
LAYERS = 1
SEQ = 256
PDIM = 4096
CAND = 128
QUERIES = 512


def with_ends(values, key, least, largest):
    index_at = [jax.random.randint(jax.random.fold_in(key, axis), (), 0, length) for axis, length in enumerate(values.shape)]
    main_axis = values.shape.index(max(values.shape))
    next_to = index_at[:main_axis] + [(index_at[main_axis] + 1) % values.shape[main_axis]] + index_at[main_axis + 1:]
    return values.at[tuple(index_at)].set(least).at[tuple(next_to)].set(largest)


def levels(key, dims, cuts, least, high):
    level, own = 1.0, jax.random.fold_in(key, 6)
    for position, parts in cuts:
        draws = jnp.exp(jax.random.uniform(jax.random.fold_in(own, position), (parts,), jnp.float32, least / len(cuts), high / len(cuts)))
        level = level * jnp.repeat(draws, dims[position] // parts).reshape([-1 if axis == position else 1 for axis in range(len(dims))])
    return level


def bell_draw(own_key, dims, width, bound, shards=(), held_as=jnp.bfloat16):
    array = jax.random.normal(own_key, dims, jnp.float32) * width
    if len(shards) > 0:
        array = levels(own_key, dims, shards, -0.22, 0.18) * array
    return jnp.clip(array, min=-bound, max=bound).astype(held_as)


def setup_inputs(seed: int = 0) -> dict:
    keys = jax.random.split(jax.random.key(seed), 7)
    return {
        "acts": bell_draw(keys[0], (LAYERS, CAND, SEQ, D), 1.0, 6.0, ((1, 8), (2, 4))),
        "out_grads": bell_draw(keys[1], (LAYERS, CAND, SEQ, D), 1.0, 6.0, ((1, 8), (2, 4))),
        "proj_in": bell_draw(keys[2], (LAYERS, D, PR), D ** -0.5, 0.09375),
        "proj_out": bell_draw(keys[3], (LAYERS, D, PR), D ** -0.5, 0.09375),
        "lengths": with_ends(jax.random.randint(keys[4], (CAND,), 1, SEQ + 1), jax.random.fold_in(keys[4], 1), 1, SEQ).astype(jnp.int32),
        "queries": bell_draw(keys[5], (QUERIES, PDIM), PDIM ** -0.5, 0.09375, ((0, 8),)),
    }


def reference(acts, out_grads, proj_in, proj_out, lengths, queries):
    positions = jnp.arange(SEQ, dtype=jnp.int32)
    masked = (positions[None, :] < lengths[:, None]).astype(jnp.float32)
    blocks = []
    for layer in range(LAYERS):
        xp = jnp.dot(acts[layer].reshape(CAND * SEQ, D), proj_in[layer], preferred_element_type=jnp.float32)
        xp = xp.astype(jnp.bfloat16).reshape(CAND, SEQ, PR)
        gp = jnp.dot(out_grads[layer].reshape(CAND * SEQ, D), proj_out[layer], preferred_element_type=jnp.float32)
        gp = gp.astype(jnp.bfloat16).reshape(CAND, SEQ, PR)
        gmask = gp.astype(jnp.float32) * masked[:, :, None]
        block = jnp.einsum('cta,ctb->cab', gmask, xp.astype(jnp.float32))
        blocks.append(block.reshape(CAND, PR * PR))
    grads = jnp.concatenate(blocks, axis=1)
    scale = lax.rsqrt(lax.optimization_barrier(jnp.mean(grads * grads, axis=1, keepdims=True)) + 1e-06)
    unit = (grads * scale).astype(jnp.bfloat16)
    return jnp.dot(unit, queries.T, preferred_element_type=jnp.float32)
```

```python
import functools

import jax
import jax.numpy as jnp
from jax import lax
from jax.experimental import pallas as pl
from jax.experimental.pallas import tpu as pltpu
from jax.sharding import PartitionSpec as P

EPS = 1e-06
NEAR = 2
F32 = jnp.float32
BF16 = jnp.bfloat16
VMEM = pl.BlockSpec(memory_space=pltpu.VMEM)
SMEM = pl.BlockSpec(memory_space=pltpu.SMEM)
ANY = pl.BlockSpec(memory_space=pl.ANY)


def team_rank(groups):
    near = lax.rem(lax.axis_index("blk"), NEAR)
    return near * groups + lax.axis_index("grp")


def grads_kernel(dims, lens, acts, out_grads, w_in, w_out, *rest):
    cands, tokens, width, team, groups, per = dims
    outs = rest[:team]
    act_buf, grad_buf, win_buf, wout_buf, square, store, sems, wsems = rest[team:]
    chunks = cands // per
    rows = per * tokens
    load_w = [
        pltpu.make_async_copy(w_out, wout_buf, wsems.at[0]),
        pltpu.make_async_copy(w_in, win_buf, wsems.at[1]),
    ]
    loads = []
    for i in range(chunks):
        part = pl.ds(i * rows, rows)
        loads.append(
            (
                pltpu.make_async_copy(out_grads.at[part], grad_buf.at[part], sems.at[0, i]),
                pltpu.make_async_copy(acts.at[part], act_buf.at[part], sems.at[1, i]),
            )
        )
    load_w[0].start()
    loads[0][0].start()
    load_w[1].start()
    loads[0][1].start()
    for pair in loads[1:]:
        for load in pair:
            load.start()
    first = lax.axis_index("grp") * tokens
    fold = 128 // width
    lines = width * width // 128
    each = lines // team
    position = lax.broadcasted_iota(jnp.int32, (tokens, width), 0) + first
    for i in range(chunks):
        part = pl.ds(i * rows, rows)
        if i == 0:
            load_w[0].wait()
        loads[i][0].wait()
        gp = jnp.dot(grad_buf[part, :], wout_buf[...], preferred_element_type=F32).astype(BF16)
        if i == 0:
            load_w[1].wait()
        loads[i][1].wait()
        xp = jnp.dot(act_buf[part, :], win_buf[...], preferred_element_type=F32).astype(BF16)
        for j in range(per):
            cand = i * per + j
            here = slice(j * tokens, (j + 1) * tokens)
            masked = jnp.where(position < lens[cand], gp[here].astype(F32), 0.0)
            block = jnp.dot(masked.T.astype(BF16), xp[here], preferred_element_type=F32)
            square[cand % 2, :, :width] = block
            line = jnp.concatenate(
                [square[cand % 2, pl.ds(h, lines, stride=fold), :width] for h in range(fold)], axis=1
            )
            for s in range(team):
                store[s, cand * each : (cand + 1) * each, :] = line[s * each : (s + 1) * each]
    rank = team_rank(groups)
    for k in range(team):
        outs[k][...] = store[jnp.bitwise_xor(rank, k)].astype(BF16)


def scores_kernel(dims, *refs):
    cands, team, groups, blks, each = dims
    parts = refs[:team]
    queries = refs[team : team + blks]
    outs = refs[team + blks : 2 * team + blks]
    grads, table, result, sems = refs[2 * team + blks :]
    nq = queries[0].shape[0]
    blk = lax.axis_index("blk")
    loads = []
    for k in range(blks):
        row = pl.multiple_of(jnp.bitwise_xor(blk, k) * nq, nq)
        loads.append(pltpu.make_async_copy(queries[k], table.at[pl.ds(row, nq)], sems.at[k]))
    for load in loads:
        load.start()
    rows = cands * each
    for half in range(NEAR):
        total = parts[half * groups][...].astype(F32)
        for g in range(1, groups):
            total = total + parts[half * groups + g][...].astype(F32)
        grads[half * rows : (half + 1) * rows, :] = total
    lines = [grads[pl.ds(e, NEAR * cands, stride=each), :] for e in range(each)]
    squares = lines[0] * lines[0]
    for line in lines[1:]:
        squares = squares + line * line
    left = jnp.concatenate([line.astype(BF16) for line in lines], axis=1)
    for load in loads:
        load.wait()
    scores = lax.dot_general(left, table[...], (((1,), (1,)), ((), ())), preferred_element_type=F32)
    owned = cands // groups
    total_q = blks * nq
    for j in range(team):
        result[j, :, :total_q] = scores[j * owned : (j + 1) * owned]
        result[j, :, total_q:] = squares[j * owned : (j + 1) * owned]
    grp = lax.axis_index("grp")
    for k in range(team):
        half, other = k // groups, k % groups
        outs[k][...] = result[half * groups + jnp.bitwise_xor(grp, other)]


def finish_kernel(pdim, *refs):
    out = refs[-1]
    total = refs[0][...]
    for ref in refs[1:-1]:
        total = total + ref[...]
    nq = out.shape[1]
    mean = jnp.sum(total[:, nq:], axis=1, keepdims=True) / pdim
    out[...] = total[:, :nq] * lax.rsqrt(mean + EPS)


def on_device(blks, groups, acts, out_grads, proj_in, proj_out, lengths, queries):
    _, cands, tokens, depth = acts.shape
    width = proj_in.shape[2]
    team = NEAR * groups
    per = 4
    pdim = width * width
    each = pdim // 128 // team
    nq = queries.shape[0]
    both = ("blk", "grp")

    def team_swap(x, k):
        near, other = k // groups, k % groups
        perm = [
            (b * groups + g, (b ^ near) * groups + (g ^ other)) for b in range(blks) for g in range(groups)
        ]
        return lax.ppermute(x, both, perm)

    slice_width = pdim // team
    rank = team_rank(groups)
    cut = [
        lax.dynamic_slice(queries, (0, jnp.bitwise_xor(rank, near * groups) * slice_width), (nq, slice_width))
        for near in range(NEAR)
    ]
    gathered = [cut[0]] + [
        lax.ppermute(cut[k % NEAR], "blk", [(b, b ^ k) for b in range(blks)]) for k in range(1, blks)
    ]

    rows = cands * tokens
    parts = pl.pallas_call(
        functools.partial(grads_kernel, (cands, tokens, width, team, groups, per)),
        out_shape=[jax.ShapeDtypeStruct((cands * each, 128), BF16)] * team,
        in_specs=[SMEM, ANY, ANY, ANY, ANY],
        out_specs=[VMEM] * team,
        scratch_shapes=[
            pltpu.VMEM((rows, depth), BF16),
            pltpu.VMEM((rows, depth), BF16),
            pltpu.VMEM((depth, width), BF16),
            pltpu.VMEM((depth, width), BF16),
            pltpu.VMEM((2, width, 128), F32),
            pltpu.VMEM((team, cands * each, 128), F32),
            pltpu.SemaphoreType.DMA((2, cands // per)),
            pltpu.SemaphoreType.DMA((2,)),
        ],
        compiler_params=pltpu.CompilerParams(vmem_limit_bytes=40 * 2**20),
        cost_estimate=pl.CostEstimate(
            flops=4 * rows * depth * width, bytes_accessed=4 * rows * depth, transcendentals=0
        ),
        name="grads",
    )(
        lengths,
        acts.reshape(rows, depth),
        out_grads.reshape(rows, depth),
        proj_in.reshape(depth, width),
        proj_out.reshape(depth, width),
    )
    parts = [parts[0]] + [team_swap(parts[k], k) for k in range(1, team)]

    owned = cands // groups
    total_q = nq * blks
    packed = jax.ShapeDtypeStruct((owned, total_q + 128), F32)
    sums = pl.pallas_call(
        functools.partial(scores_kernel, (cands, team, groups, blks, each)),
        out_shape=[packed] * team,
        in_specs=[VMEM] * team + [ANY] * blks,
        out_specs=[VMEM] * team,
        scratch_shapes=[
            pltpu.VMEM((NEAR * cands * each, 128), F32),
            pltpu.VMEM((total_q, slice_width), BF16),
            pltpu.VMEM((team, owned, total_q + 128), F32),
            pltpu.SemaphoreType.DMA((blks,)),
        ],
        compiler_params=pltpu.CompilerParams(vmem_limit_bytes=24 * 2**20),
        cost_estimate=pl.CostEstimate(
            flops=2 * NEAR * cands * total_q * slice_width,
            bytes_accessed=2 * total_q * slice_width,
            transcendentals=0,
        ),
        name="scores",
    )(*parts, *gathered)
    sums = [sums[0]] + [team_swap(sums[k], k) for k in range(1, team)]

    return pl.pallas_call(
        functools.partial(finish_kernel, pdim),
        out_shape=jax.ShapeDtypeStruct((owned, total_q), F32),
        in_specs=[VMEM] * team,
        out_specs=VMEM,
        name="finish",
    )(*sums)


def solution(mesh):
    in_specs = (
        P(None, "blk", "grp", None),
        P(None, "blk", "grp", None),
        P(),
        P(),
        P("blk"),
        P("blk", None),
    )
    return jax.shard_map(
        functools.partial(on_device, mesh.shape["blk"], mesh.shape["grp"]),
        mesh=mesh,
        in_specs=in_specs,
        out_specs=P(("blk", "grp"), None),
        check_vma=False,
    )
```

```python
import functools

import jax
import jax.numpy as jnp
from jax import lax
from jax.experimental import pallas as pl
from jax.experimental.pallas import tpu as pltpu
from jax.sharding import Mesh
from jax.sharding import PartitionSpec as P

EPS = 1e-06
NEAR = 2
F32 = jnp.float32
BF16 = jnp.bfloat16
VMEM = pl.BlockSpec(memory_space=pltpu.VMEM)
ANY = pl.BlockSpec(memory_space=pl.ANY)


def grads_kernel(dims, lens_in, acts, out_grads, w_in, w_out, out, *rest):
    cands, tokens, width, team, per = dims
    act_buf, grad_buf, win_buf, wout_buf, lens, square, store, sems, wsems = rest
    chunks = cands // per
    rows = per * tokens
    load_lens = pltpu.make_async_copy(lens_in, lens, wsems.at[2])
    load_w = [
        pltpu.make_async_copy(w_out, wout_buf, wsems.at[0]),
        pltpu.make_async_copy(w_in, win_buf, wsems.at[1]),
    ]
    loads = []
    for i in range(chunks):
        part = pl.ds(i * rows, rows)
        loads.append(
            (
                pltpu.make_async_copy(out_grads.at[part], grad_buf.at[part], sems.at[0, i]),
                pltpu.make_async_copy(acts.at[part], act_buf.at[part], sems.at[1, i]),
            )
        )
    load_w[0].start()
    loads[0][0].start()
    load_w[1].start()
    loads[0][1].start()
    load_lens.start()
    for pair in loads[1:]:
        for load in pair:
            load.start()
    first = lax.axis_index("grp") * tokens
    fold = 128 // width
    lines = width * width // 128
    each = lines // team
    position = lax.broadcasted_iota(jnp.int32, (tokens, width), 0) + first
    transposed = (((1,), (1,)), ((), ()))
    for i in range(chunks):
        part = pl.ds(i * rows, rows)
        if i == 0:
            load_w[0].wait()
        loads[i][0].wait()
        gp = lax.dot_general(grad_buf[part, :], wout_buf[...], transposed, preferred_element_type=F32)
        gp = gp.astype(BF16)
        if i == 0:
            load_w[1].wait()
            load_lens.wait()
        loads[i][1].wait()
        xp = lax.dot_general(act_buf[part, :], win_buf[...], transposed, preferred_element_type=F32)
        xp = xp.astype(BF16)
        for j in range(per):
            cand = i * per + j
            here = slice(j * tokens, (j + 1) * tokens)
            masked = jnp.where(position < lens[cand], gp[here].astype(F32), 0.0)
            block = jnp.dot(masked.T.astype(BF16), xp[here], preferred_element_type=F32)
            square[cand % 2, :, :width] = block
            line = jnp.concatenate(
                [square[cand % 2, pl.ds(h, lines, stride=fold), :width] for h in range(fold)], axis=1
            )
            for s in range(team):
                store[s, cand * each : (cand + 1) * each, :] = line[s * each : (s + 1) * each]
    out[...] = store[...].astype(BF16)


def scores_kernel(dims, parts, queries, out, grads):
    cands, team, groups, each = dims
    rows = cands * each
    for half in range(NEAR):
        total = parts[half * groups].astype(F32)
        for g in range(1, groups):
            total = total + parts[half * groups + g].astype(F32)
        grads[half * rows : (half + 1) * rows, :] = total
    lines = [grads[pl.ds(e, NEAR * cands, stride=each), :] for e in range(each)]
    squares = lines[0] * lines[0]
    for line in lines[1:]:
        squares = squares + line * line
    left = jnp.concatenate([line.astype(BF16) for line in lines], axis=1)
    scores = lax.dot_general(left, queries[...], (((1,), (1,)), ((), ())), preferred_element_type=F32)
    owned = cands // groups
    nq = queries.shape[0]
    for j in range(team):
        out[j, :, :nq] = scores[j * owned : (j + 1) * owned]
        out[j, :, nq:] = squares[j * owned : (j + 1) * owned]


def finish_kernel(pdim, parts, out):
    total = parts[0]
    for k in range(1, parts.shape[0]):
        total = total + parts[k]
    nq = out.shape[1]
    mean = jnp.sum(total[:, nq:], axis=1, keepdims=True) / pdim
    out[...] = total[:, :nq] * lax.rsqrt(mean + EPS)


def on_device(acts, out_grads, proj_in, proj_out, lengths, queries):
    _, cands, tokens, depth = acts.shape
    far, groups = lax.axis_size("far"), lax.axis_size("grp")
    width = proj_in.shape[2]
    team = NEAR * groups
    per = 4
    pdim = width * width
    each = pdim // 128 // team
    nq = queries.shape[0]
    total_q = nq * far * NEAR
    slice_width = pdim // team
    grp = lax.axis_index("grp")
    cut = jnp.stack(
        [
            lax.dynamic_slice(queries, (0, (near * groups + grp) * slice_width), (nq, slice_width))
            for near in range(NEAR)
        ]
    )
    cut = jnp.broadcast_to(cut[None], (far, NEAR, nq, slice_width)).reshape(far * NEAR, nq, slice_width)
    gathered = lax.all_to_all(cut, ("far", "near"), 0, 0, tiled=True).reshape(total_q, slice_width)

    rows = cands * tokens
    parts = pl.pallas_call(
        functools.partial(grads_kernel, (cands, tokens, width, team, per)),
        out_shape=jax.ShapeDtypeStruct((team, cands * each, 128), BF16),
        in_specs=[ANY] * 5,
        out_specs=VMEM,
        scratch_shapes=[
            pltpu.VMEM((rows, depth), BF16),
            pltpu.VMEM((rows, depth), BF16),
            pltpu.VMEM((width, depth), BF16),
            pltpu.VMEM((width, depth), BF16),
            pltpu.SMEM((cands,), jnp.int32),
            pltpu.VMEM((2, width, 128), F32),
            pltpu.VMEM((team, cands * each, 128), F32),
            pltpu.SemaphoreType.DMA((2, cands // per)),
            pltpu.SemaphoreType.DMA((3,)),
        ],
        compiler_params=pltpu.CompilerParams(vmem_limit_bytes=58 * 2**20),
        cost_estimate=pl.CostEstimate(
            flops=4 * rows * depth * width, bytes_accessed=4 * rows * depth, transcendentals=0
        ),
        name="grads",
    )(
        lengths,
        acts.reshape(rows, depth),
        out_grads.reshape(rows, depth),
        proj_in.reshape(depth, width).T,
        proj_out.reshape(depth, width).T,
    )
    parts = lax.all_to_all(parts, ("near", "grp"), 0, 0, tiled=True)

    owned = cands // groups
    sums = pl.pallas_call(
        functools.partial(scores_kernel, (cands, team, groups, each)),
        out_shape=jax.ShapeDtypeStruct((team, owned, total_q + 128), F32),
        in_specs=[VMEM] * 2,
        out_specs=VMEM,
        scratch_shapes=[pltpu.VMEM((NEAR * cands * each, 128), F32)],
        compiler_params=pltpu.CompilerParams(vmem_limit_bytes=24 * 2**20),
        cost_estimate=pl.CostEstimate(
            flops=2 * NEAR * cands * total_q * slice_width,
            bytes_accessed=2 * total_q * slice_width,
            transcendentals=0,
        ),
        name="scores",
    )(parts, gathered)
    sums = lax.all_to_all(sums, ("near", "grp"), 0, 0, tiled=True)

    return pl.pallas_call(
        functools.partial(finish_kernel, pdim),
        out_shape=jax.ShapeDtypeStruct((owned, total_q), F32),
        in_specs=[VMEM],
        out_specs=VMEM,
        name="finish",
    )(sums)


def solution(mesh):
    blks, groups = mesh.shape["blk"], mesh.shape["grp"]
    fine = Mesh(mesh.devices.reshape(blks // NEAR, NEAR, groups), ("far", "near", "grp"))
    blk = ("far", "near")
    in_specs = (
        P(None, blk, "grp", None),
        P(None, blk, "grp", None),
        P(),
        P(),
        P(blk),
        P(blk, None),
    )
    return jax.shard_map(
        on_device, mesh=fine, in_specs=in_specs, out_specs=P(blk + ("grp",), None), check_vma=False
    )
```

```python
import functools

import jax
import jax.numpy as jnp
from jax import lax
from jax.experimental import pallas as pl
from jax.experimental.pallas import tpu as pltpu
from jax.sharding import PartitionSpec as P

EPS = 1e-06
F32 = jnp.float32
BF16 = jnp.bfloat16
VMEM = pl.BlockSpec(memory_space=pltpu.VMEM)
ANY = pl.BlockSpec(memory_space=pl.ANY)
BY_ROWS = (((1,), (1,)), ((), ()))


def grads_kernel(dims, lens_in, acts, out_grads, w_in, w_out, *rest):
    cands, tokens, width, groups, per = dims
    outs = rest[:groups]
    act_buf, grad_buf, win_raw, wout_raw, win_buf, wout_buf, lens, square, store, sems, wsems = rest[groups:]
    chunks = cands // per
    rows = per * tokens
    load_lens = pltpu.make_async_copy(lens_in, lens, wsems.at[2])
    load_w = [
        pltpu.make_async_copy(w_out, wout_raw, wsems.at[0]),
        pltpu.make_async_copy(w_in, win_raw, wsems.at[1]),
    ]
    loads = []
    for i in range(chunks):
        part = pl.ds(i * rows, rows)
        loads.append(
            (
                pltpu.make_async_copy(out_grads.at[part], grad_buf.at[part], sems.at[0, i]),
                pltpu.make_async_copy(acts.at[part], act_buf.at[part], sems.at[1, i]),
            )
        )
    for load in load_w:
        load.start()
    load_lens.start()
    for pair in loads:
        for load in pair:
            load.start()
    grp = lax.axis_index("grp")
    fold = 128 // width
    lines = width * width // 128
    each = lines // groups
    position = lax.broadcasted_iota(jnp.int32, (tokens, width), 0) + grp * tokens
    load_w[0].wait()
    wout_buf[...] = wout_raw[...].T
    load_w[1].wait()
    win_buf[...] = win_raw[...].T
    load_lens.wait()
    for i in range(chunks):
        part = pl.ds(i * rows, rows)
        loads[i][0].wait()
        gp = jnp.dot(grad_buf[part, :], wout_buf[...], preferred_element_type=F32).astype(BF16)
        loads[i][1].wait()
        xp = jnp.dot(act_buf[part, :], win_buf[...], preferred_element_type=F32).astype(BF16)
        for j in range(per):
            cand = i * per + j
            here = slice(j * tokens, (j + 1) * tokens)
            masked = jnp.where(position < lens[cand], gp[here].astype(F32), 0.0)
            block = jnp.dot(masked.T.astype(BF16), xp[here], preferred_element_type=F32)
            square[cand % 2, :, :width] = block
            line = jnp.concatenate(
                [square[cand % 2, pl.ds(h, lines, stride=fold), :width] for h in range(fold)], axis=1
            )
            for s in range(groups):
                store[s, cand * each : (cand + 1) * each, :] = line[s * each : (s + 1) * each]
    for k in range(groups):
        outs[k][...] = store[jnp.bitwise_xor(grp, k)].astype(BF16)


def combine_kernel(dims, *refs):
    cands, groups, each = dims
    parts = refs[:groups]
    out, squares, grads = refs[groups:]
    total = parts[0][...].astype(F32)
    for part in parts[1:]:
        total = total + part[...].astype(F32)
    grads[...] = total
    lines = [grads[pl.ds(e, cands, stride=each), :] for e in range(each)]
    sums = lines[0] * lines[0]
    for line in lines[1:]:
        sums = sums + line * line
    squares[...] = sums
    out[...] = jnp.concatenate([line.astype(BF16) for line in lines], axis=1)


def near_scores(left, queries, place):
    far = len(queries)
    z = lax.axis_index("blk") // 2
    for k in range(far):
        place[jnp.bitwise_xor(z, k)] = lax.dot_general(
            left, queries[k][...], BY_ROWS, preferred_element_type=F32
        )
    return jnp.concatenate([place[k] for k in range(far)], axis=1)


def other_kernel(far, left, *refs):
    refs[far][...] = near_scores(left[...], refs[:far], refs[far + 1])


def own_kernel(dims, left, squares, *refs):
    far, groups = dims
    queries = refs[:far]
    other = refs[far]
    outs = refs[far + 1 : far + 1 + groups]
    place, result = refs[far + 1 + groups :]
    own = near_scores(left[...], queries, place)
    is_even = lax.rem(lax.axis_index("blk"), 2) == 0
    back = other[...]
    even = jnp.where(is_even, own, back)
    odd = jnp.where(is_even, back, own)
    half = own.shape[1]
    owned = own.shape[0] // groups
    for g in range(groups):
        here = slice(g * owned, (g + 1) * owned)
        result[g, :, :half] = even[here]
        result[g, :, half : 2 * half] = odd[here]
        result[g, :, 2 * half :] = squares[here, :]
    grp = lax.axis_index("grp")
    for k in range(groups):
        outs[k][...] = result[jnp.bitwise_xor(grp, k)]


def finish_kernel(dims, *refs):
    pdim, nq = dims
    out = refs[-1]
    total = refs[0][...]
    for ref in refs[1:-1]:
        total = total + ref[...]
    width = out.shape[1]
    mean = jnp.sum(total[:, width:], axis=1, keepdims=True) / pdim
    scaled = total[:, :width] * lax.rsqrt(mean + EPS)
    columns = []
    for start in range(0, width // 2, nq):
        columns.append(scaled[:, start : start + nq])
        columns.append(scaled[:, width // 2 + start : width // 2 + start + nq])
    out[...] = jnp.concatenate(columns, axis=1)


def on_device(blks, groups, acts, out_grads, proj_in, proj_out, lengths, queries):
    _, cands, tokens, depth = acts.shape
    width = proj_in.shape[2]
    per = 4
    far = blks // 2
    pdim = width * width
    each = pdim // 128 // groups
    nq = queries.shape[0]
    total_q = nq * blks
    owned = cands // groups
    slice_width = pdim // groups

    def grp_swap(x, k):
        return lax.ppermute(x, "grp", [(g, g ^ k) for g in range(groups)])

    def blk_swap(x, k):
        return lax.ppermute(x, "blk", [(b, b ^ k) for b in range(blks)])

    cut = lax.dynamic_slice(queries, (0, lax.axis_index("grp") * slice_width), (nq, slice_width))
    gathered = [cut] + [blk_swap(cut, 2 * k) for k in range(1, far)]

    rows = cands * tokens
    parts = pl.pallas_call(
        functools.partial(grads_kernel, (cands, tokens, width, groups, per)),
        out_shape=[jax.ShapeDtypeStruct((cands * each, 128), BF16)] * groups,
        in_specs=[ANY] * 5,
        out_specs=[VMEM] * groups,
        scratch_shapes=[
            pltpu.VMEM((rows, depth), BF16),
            pltpu.VMEM((rows, depth), BF16),
            pltpu.VMEM((width, depth), BF16),
            pltpu.VMEM((width, depth), BF16),
            pltpu.VMEM((depth, width), BF16),
            pltpu.VMEM((depth, width), BF16),
            pltpu.SMEM((cands,), jnp.int32),
            pltpu.VMEM((2, width, 128), F32),
            pltpu.VMEM((groups, cands * each, 128), F32),
            pltpu.SemaphoreType.DMA((2, cands // per)),
            pltpu.SemaphoreType.DMA((3,)),
        ],
        compiler_params=pltpu.CompilerParams(vmem_limit_bytes=58 * 2**20),
        cost_estimate=pl.CostEstimate(
            flops=16 * rows * depth * width, bytes_accessed=8 * rows * depth, transcendentals=0
        ),
        name="grads",
    )(
        lengths,
        acts.reshape(rows, depth),
        out_grads.reshape(rows, depth),
        proj_in.reshape(depth, width).T,
        proj_out.reshape(depth, width).T,
    )
    parts = [parts[0]] + [grp_swap(parts[k], k) for k in range(1, groups)]

    own, squares = pl.pallas_call(
        functools.partial(combine_kernel, (cands, groups, each)),
        out_shape=[
            jax.ShapeDtypeStruct((cands, slice_width), BF16),
            jax.ShapeDtypeStruct((cands, 128), F32),
        ],
        in_specs=[VMEM] * groups,
        out_specs=[VMEM] * 2,
        scratch_shapes=[pltpu.VMEM((cands * each, 128), F32)],
        name="combine",
    )(*parts)
    neighbour = blk_swap(own, 1)

    half = total_q // 2
    place = pltpu.VMEM((far, cands, nq), F32)
    back = pl.pallas_call(
        functools.partial(other_kernel, far),
        out_shape=jax.ShapeDtypeStruct((cands, half), F32),
        in_specs=[VMEM] * (1 + far),
        out_specs=VMEM,
        scratch_shapes=[place],
        compiler_params=pltpu.CompilerParams(vmem_limit_bytes=24 * 2**20),
        name="other_scores",
    )(neighbour, *gathered)
    back = blk_swap(back, 1)

    packed = jax.ShapeDtypeStruct((owned, total_q + 128), F32)
    sums = pl.pallas_call(
        functools.partial(own_kernel, (far, groups)),
        out_shape=[packed] * groups,
        in_specs=[VMEM] * (3 + far),
        out_specs=[VMEM] * groups,
        scratch_shapes=[place, pltpu.VMEM((groups, owned, total_q + 128), F32)],
        compiler_params=pltpu.CompilerParams(vmem_limit_bytes=24 * 2**20),
        name="own_scores",
    )(own, squares, *gathered, back)
    sums = [sums[0]] + [grp_swap(sums[k], k) for k in range(1, groups)]

    return pl.pallas_call(
        functools.partial(finish_kernel, (pdim, nq)),
        out_shape=jax.ShapeDtypeStruct((owned, total_q), F32),
        in_specs=[VMEM] * groups,
        out_specs=VMEM,
        name="finish",
    )(*sums)


def solution(mesh):
    in_specs = (
        P(None, "blk", "grp", None),
        P(None, "blk", "grp", None),
        P(),
        P(),
        P("blk"),
        P("blk", None),
    )
    return jax.shard_map(
        functools.partial(on_device, mesh.shape["blk"], mesh.shape["grp"]),
        mesh=mesh,
        in_specs=in_specs,
        out_specs=P(("blk", "grp"), None),
        check_vma=False,
    )
```

```python
import functools

import jax
import jax.numpy as jnp
from jax import lax
from jax.experimental import pallas as pl
from jax.experimental.pallas import tpu as pltpu
from jax.sharding import PartitionSpec as P

EPS = 1e-06
F32 = jnp.float32
BF16 = jnp.bfloat16
VMEM = pl.BlockSpec(memory_space=pltpu.VMEM)
HBM = pl.BlockSpec(memory_space=pltpu.HBM)
BY_ROWS = (((1,), (1,)), ((), ()))


def grads_kernel(dims, lens_in, acts, out_grads, w_in, w_out, send, keep, *rest):
    cands, tokens, width, groups = dims
    act_buf, grad_buf, win_raw, wout_raw, win_buf, wout_buf, lens, store, sems, wsems = rest
    half = cands // 2
    chunks = half // 2
    rows = 4 * tokens
    load_lens = pltpu.make_async_copy(lens_in, lens, wsems.at[2])
    load_w = [
        pltpu.make_async_copy(w_out, wout_raw, wsems.at[0]),
        pltpu.make_async_copy(w_in, win_raw, wsems.at[1]),
    ]
    loads = []
    for i in range(chunks):
        for side, (source, buf) in enumerate(((out_grads, grad_buf), (acts, act_buf))):
            loads.append(
                [
                    pltpu.make_async_copy(
                        source.at[pl.ds((2 * i + h * half) * tokens, rows // 2)],
                        buf.at[pl.ds(i * rows + h * (rows // 2), rows // 2)],
                        sems.at[side, 2 * i + h],
                    )
                    for h in range(2)
                ]
            )
    load_w[0].start()
    load_w[1].start()
    load_lens.start()
    for pair in loads:
        for load in pair:
            load.start()
    grp = lax.axis_index("grp")
    lines = width // groups
    position = lax.broadcasted_iota(jnp.int32, (tokens, width), 0) + grp * tokens
    row_blk = lax.broadcasted_iota(jnp.int32, (rows, rows), 0) // tokens
    col_blk = lax.broadcasted_iota(jnp.int32, (rows, 4 * width), 1) // width
    diagonal = row_blk == col_blk // 2 + 2 * (col_blk % 2)
    load_w[0].wait()
    wout_buf[...] = wout_raw[...].T
    load_w[1].wait()
    load_lens.wait()
    for i in range(chunks):
        part = pl.ds(i * rows, rows)
        for load in loads[2 * i]:
            load.wait()
        gp = jnp.dot(grad_buf[part, :], wout_buf[...], preferred_element_type=F32)
        if i == 0:
            win_buf[...] = win_raw[...].T
        left = gp.T.astype(BF16)
        for load in loads[2 * i + 1]:
            load.wait()
        xp = jnp.dot(act_buf[part, :], win_buf[...], preferred_element_type=F32)
        used = []
        for j in range(4):
            cand = 2 * i + j % 2 + (j // 2) * half
            used.append(jnp.where(position < lens[cand], xp[j * tokens : (j + 1) * tokens], 0.0))
        wide = jnp.concatenate([jnp.concatenate(used, axis=0)] * 4, axis=1)
        right = jnp.where(diagonal, wide, 0.0).astype(BF16)
        blocks = jnp.dot(left, right, preferred_element_type=F32)
        for t in range(2):
            pair = 2 * i + t
            for s in range(groups):
                store[s, pair * lines : (pair + 1) * lines, :] = blocks[
                    s * lines : (s + 1) * lines, t * 128 : (t + 1) * 128
                ]
    core = lax.rem(grp, 2)
    for x in range(groups // 2):
        send[x] = store[2 * x + 1 - core].astype(BF16)
        keep[x] = store[2 * x + core]


def fold_kernel(keep, came, send, kept):
    x = lax.axis_index("grp") // 2
    send[...] = (keep[1 - x] + came[1 - x].astype(F32)).astype(BF16)
    kept[...] = keep[x] + came[x].astype(F32)


def combine_kernel(dims, kept, came, out, squares, grads):
    half, lines, width = dims
    grads[...] = kept[...] + came[...].astype(F32)
    low = lax.broadcasted_iota(jnp.int32, (half, 128), 1) < width
    sums, columns = None, []
    for e in range(0, lines, 2):
        first = grads[pl.ds(e, half, stride=lines), :]
        second = grads[pl.ds(e + 1, half, stride=lines), :]
        line = jnp.concatenate(
            [
                jnp.where(low, first, pltpu.roll(second, width, 1)),
                jnp.where(low, pltpu.roll(first, width, 1), second),
            ],
            axis=0,
        )
        columns.append(line.astype(BF16))
        sums = line * line if sums is None else sums + line * line
    squares[...] = sums
    out[...] = jnp.concatenate(columns, axis=1)


def near_scores(left, queries, place):
    far = len(queries)
    z = lax.axis_index("blk") // 2
    for k in range(far):
        place[jnp.bitwise_xor(z, k)] = lax.dot_general(
            left, queries[k][...], BY_ROWS, preferred_element_type=F32
        )
    return jnp.concatenate([place[k] for k in range(far)], axis=1)


def other_kernel(far, left, *refs):
    refs[far][...] = near_scores(left[...], refs[:far], refs[far + 1])


def own_kernel(dims, left, squares, *refs):
    far, groups = dims
    queries = refs[:far]
    other, send, keep, place, result = refs[far:]
    own = near_scores(left[...], queries, place)
    is_even = lax.rem(lax.axis_index("blk"), 2) == 0
    back = other[...]
    even = jnp.where(is_even, own, back)
    odd = jnp.where(is_even, back, own)
    half = own.shape[1]
    owned = own.shape[0] // groups
    for g in range(groups):
        here = slice(g * owned, (g + 1) * owned)
        result[g, :, :half] = even[here]
        result[g, :, half : 2 * half] = odd[here]
        result[g, :, 2 * half :] = squares[here, :]
    x = lax.axis_index("grp") // 2
    for core in range(2):
        send[core] = result[2 * (1 - x) + core]
        keep[core] = result[2 * x + core]


def pass_kernel(keep, came, send, kept):
    core = lax.rem(lax.axis_index("grp"), 2)
    send[...] = keep[1 - core] + came[1 - core]
    kept[...] = keep[core] + came[core]


def finish_kernel(dims, kept, came, out):
    pdim, nq = dims
    total = kept[...] + came[...]
    width = out.shape[1]
    mean = jnp.sum(total[:, width:], axis=1, keepdims=True) / pdim
    scaled = total[:, :width] * lax.rsqrt(mean + EPS)
    columns = []
    for start in range(0, width // 2, nq):
        columns.append(scaled[:, start : start + nq])
        columns.append(scaled[:, width // 2 + start : width // 2 + start + nq])
    out[...] = jnp.concatenate(columns, axis=1)


def small(kernel, out_shape, operands, scratch_shapes=(), name=None):
    one = not isinstance(out_shape, list)
    return pl.pallas_call(
        kernel,
        out_shape=out_shape,
        in_specs=[VMEM] * len(operands),
        out_specs=VMEM if one else [VMEM] * len(out_shape),
        scratch_shapes=list(scratch_shapes),
        compiler_params=pltpu.CompilerParams(vmem_limit_bytes=16 * 2**20),
        name=name,
    )(*operands)


def on_device(blks, groups, acts, out_grads, proj_in, proj_out, lengths, queries):
    _, cands, tokens, depth = acts.shape
    width = proj_in.shape[2]
    far = blks // 2
    pdim = width * width
    lines = width // groups
    nq = queries.shape[0]
    total_q = nq * blks
    owned = cands // groups
    slice_width = pdim // groups
    shape = jax.ShapeDtypeStruct

    def grp_swap(x, k):
        return lax.ppermute(x, "grp", [(g, g ^ k) for g in range(groups)])

    def blk_swap(x, k):
        return lax.ppermute(x, "blk", [(b, b ^ k) for b in range(blks)])

    cut = lax.dynamic_slice(queries, (0, lax.axis_index("grp") * slice_width), (nq, slice_width))
    gathered = [cut] + [blk_swap(cut, 2 * k) for k in range(1, far)]

    rows = cands * tokens
    piece = (cands // 2 * lines, 128)
    send, keep = pl.pallas_call(
        functools.partial(grads_kernel, (cands, tokens, width, groups)),
        out_shape=[shape((groups // 2,) + piece, BF16), shape((groups // 2,) + piece, F32)],
        in_specs=[HBM] * 5,
        out_specs=[VMEM] * 2,
        scratch_shapes=[
            pltpu.VMEM((rows, depth), BF16),
            pltpu.VMEM((rows, depth), BF16),
            pltpu.VMEM((width, depth), BF16),
            pltpu.VMEM((width, depth), BF16),
            pltpu.VMEM((depth, width), BF16),
            pltpu.VMEM((depth, width), BF16),
            pltpu.SMEM((cands,), jnp.int32),
            pltpu.VMEM((groups,) + piece, F32),
            pltpu.SemaphoreType.DMA((2, cands // 2)),
            pltpu.SemaphoreType.DMA((3,)),
        ],
        compiler_params=pltpu.CompilerParams(vmem_limit_bytes=54784 * 2**10),
        cost_estimate=pl.CostEstimate(
            flops=16 * rows * depth * width, bytes_accessed=8 * rows * depth, transcendentals=0
        ),
        name="grads",
    )(
        lengths,
        acts.reshape(rows, depth),
        out_grads.reshape(rows, depth),
        proj_in.reshape(depth, width).T,
        proj_out.reshape(depth, width).T,
    )
    send, kept = small(
        fold_kernel, [shape(piece, BF16), shape(piece, F32)], (keep, grp_swap(send, 1)), name="fold"
    )
    own, squares = small(
        functools.partial(combine_kernel, (cands // 2, lines, width)),
        [shape((cands, slice_width), BF16), shape((cands, 128), F32)],
        (kept, grp_swap(send, 2)),
        [pltpu.VMEM(piece, F32)],
        name="combine",
    )
    place = pltpu.VMEM((far, cands, nq), F32)
    back = small(
        functools.partial(other_kernel, far),
        shape((cands, total_q // 2), F32),
        (blk_swap(own, 1), *gathered),
        [place],
        name="other_scores",
    )
    line = (owned, total_q + 128)
    send, keep = small(
        functools.partial(own_kernel, (far, groups)),
        [shape((groups // 2,) + line, F32)] * 2,
        (own, squares, *gathered, blk_swap(back, 1)),
        [place, pltpu.VMEM((groups,) + line, F32)],
        name="own_scores",
    )
    send, kept = small(pass_kernel, [shape(line, F32)] * 2, (keep, grp_swap(send, 2)), name="pass")
    return small(
        functools.partial(finish_kernel, (pdim, nq)),
        shape((owned, total_q), F32),
        (kept, grp_swap(send, 1)),
        name="finish",
    )


def solution(mesh):
    in_specs = (
        P(None, "blk", "grp", None),
        P(None, "blk", "grp", None),
        P(),
        P(),
        P("blk"),
        P("blk", None),
    )
    return jax.shard_map(
        functools.partial(on_device, mesh.shape["blk"], mesh.shape["grp"]),
        mesh=mesh,
        in_specs=in_specs,
        out_specs=P(("blk", "grp"), None),
        check_vma=False,
    )
```

```python
import functools

import jax
import jax.numpy as jnp
from jax import lax
from jax.experimental import pallas as pl
from jax.experimental.pallas import tpu as pltpu
from jax.sharding import PartitionSpec as P

EPS = 1e-06
F32 = jnp.float32
BF16 = jnp.bfloat16
VMEM = pl.BlockSpec(memory_space=pltpu.VMEM)
SMEM = pl.BlockSpec(memory_space=pltpu.SMEM)
BY_ROWS = (((1,), (1,)), ((), ()))


def grads_kernel(dims, lens, xp_in, gp_in, send, keep, store):
    cands, tokens, width, groups = dims
    half = cands // 2
    rows = 4 * tokens
    grp = lax.axis_index("grp")
    lines = width // groups
    position = lax.broadcasted_iota(jnp.int32, (tokens, width), 0) + grp * tokens
    row_blk = lax.broadcasted_iota(jnp.int32, (rows, rows), 0) // tokens
    col_blk = lax.broadcasted_iota(jnp.int32, (rows, 4 * width), 1) // width
    diagonal = row_blk == col_blk // 2 + 2 * (col_blk % 2)
    for i in range(half // 2):
        members = [2 * i, 2 * i + 1, 2 * i + half, 2 * i + 1 + half]
        parts = [slice(cand * tokens, (cand + 2) * tokens) for cand in members[::2]]
        left = jnp.concatenate([gp_in[:, part] for part in parts], axis=1)
        xp = jnp.concatenate([xp_in[:, part].astype(F32).T for part in parts], axis=0)
        used = [
            jnp.where(position < lens[cand], xp[j * tokens : (j + 1) * tokens], 0.0)
            for j, cand in enumerate(members)
        ]
        wide = jnp.concatenate([jnp.concatenate(used, axis=0)] * 4, axis=1)
        right = jnp.where(diagonal, wide, 0.0).astype(BF16)
        blocks = jnp.dot(left, right, preferred_element_type=F32)
        for t in range(2):
            pair = 2 * i + t
            for s in range(groups):
                store[s, pair * lines : (pair + 1) * lines, :] = blocks[
                    s * lines : (s + 1) * lines, t * 128 : (t + 1) * 128
                ]
    core = lax.rem(grp, 2)
    for x in range(groups // 2):
        send[x] = store[2 * x + 1 - core].astype(BF16)
        keep[x] = store[2 * x + core]


def fold_kernel(keep, came, *rest):
    send, kept = rest[-2:]
    x = lax.axis_index("grp") // 2
    send[...] = (keep[1 - x] + came[1 - x].astype(F32)).astype(BF16)
    kept[...] = keep[x] + came[x].astype(F32)


def combine_kernel(dims, kept, came, out, squares, grads):
    half, lines, width = dims
    grads[...] = kept[...] + came[...].astype(F32)
    low = lax.broadcasted_iota(jnp.int32, (half, 128), 1) < width
    sums, columns = None, []
    for e in range(0, lines, 2):
        first = grads[pl.ds(e, half, stride=lines), :]
        second = grads[pl.ds(e + 1, half, stride=lines), :]
        line = jnp.concatenate(
            [
                jnp.where(low, first, pltpu.roll(second, width, 1)),
                jnp.where(low, pltpu.roll(first, width, 1), second),
            ],
            axis=0,
        )
        columns.append(line.astype(BF16))
        sums = line * line if sums is None else sums + line * line
    squares[...] = sums
    out[...] = jnp.concatenate(columns, axis=1)


def near_scores(left, queries, place):
    far = len(queries)
    z = lax.axis_index("blk") // 2
    for k in range(far):
        place[jnp.bitwise_xor(z, k)] = lax.dot_general(
            left, queries[k][...], BY_ROWS, preferred_element_type=F32
        )
    return jnp.concatenate([place[k] for k in range(far)], axis=1)


def other_kernel(far, left, *refs):
    refs[far][...] = near_scores(left[...], refs[:far], refs[far + 1])


def own_kernel(dims, left, squares, *refs):
    far, groups = dims
    queries = refs[:far]
    other, send, keep, place, result = refs[far:]
    own = near_scores(left[...], queries, place)
    is_even = lax.rem(lax.axis_index("blk"), 2) == 0
    back = other[...]
    even = jnp.where(is_even, own, back)
    odd = jnp.where(is_even, back, own)
    half = own.shape[1]
    owned = own.shape[0] // groups
    for g in range(groups):
        here = slice(g * owned, (g + 1) * owned)
        result[g, :, :half] = even[here]
        result[g, :, half : 2 * half] = odd[here]
        result[g, :, 2 * half :] = squares[here, :]
    x = lax.axis_index("grp") // 2
    for core in range(2):
        send[core] = result[2 * (1 - x) + core]
        keep[core] = result[2 * x + core]


def pass_kernel(keep, came, send, kept):
    core = lax.rem(lax.axis_index("grp"), 2)
    send[...] = keep[1 - core] + came[1 - core]
    kept[...] = keep[core] + came[core]


def finish_kernel(dims, kept, came, out):
    pdim, nq = dims
    total = kept[...] + came[...]
    width = out.shape[1]
    mean = jnp.sum(total[:, width:], axis=1, keepdims=True) / pdim
    scaled = total[:, :width] * lax.rsqrt(mean + EPS)
    columns = []
    for start in range(0, width // 2, nq):
        columns.append(scaled[:, start : start + nq])
        columns.append(scaled[:, width // 2 + start : width // 2 + start + nq])
    out[...] = jnp.concatenate(columns, axis=1)


def small(kernel, out_shape, operands, scratch_shapes=(), name=None, first=VMEM):
    one = not isinstance(out_shape, list)
    return pl.pallas_call(
        kernel,
        out_shape=out_shape,
        in_specs=[first] + [VMEM] * (len(operands) - 1),
        out_specs=VMEM if one else [VMEM] * len(out_shape),
        scratch_shapes=list(scratch_shapes),
        compiler_params=pltpu.CompilerParams(vmem_limit_bytes=16 * 2**20),
        name=name,
    )(*operands)


def on_device(blks, groups, acts, out_grads, proj_in, proj_out, lengths, queries):
    _, cands, tokens, depth = acts.shape
    width = proj_in.shape[2]
    far = blks // 2
    pdim = width * width
    lines = width // groups
    nq = queries.shape[0]
    total_q = nq * blks
    owned = cands // groups
    slice_width = pdim // groups
    shape = jax.ShapeDtypeStruct

    def grp_swap(x, k):
        return lax.ppermute(x, "grp", [(g, g ^ k) for g in range(groups)])

    def blk_swap(x, k):
        return lax.ppermute(x, "blk", [(b, b ^ k) for b in range(blks)])

    cut = lax.dynamic_slice(queries, (0, lax.axis_index("grp") * slice_width), (nq, slice_width))
    gathered = [cut] + [blk_swap(cut, 2 * k) for k in range(1, far)]

    rows = cands * tokens
    piece = (cands // 2 * lines, 128)
    gp = jnp.dot(out_grads.reshape(rows, depth), proj_out[0], preferred_element_type=F32).astype(BF16)
    xp = jnp.dot(acts.reshape(rows, depth), proj_in[0], preferred_element_type=F32).astype(BF16)
    send, keep = small(
        functools.partial(grads_kernel, (cands, tokens, width, groups)),
        [shape((groups // 2,) + piece, BF16), shape((groups // 2,) + piece, F32)],
        (lengths, xp.T, gp.T),
        [pltpu.VMEM((groups,) + piece, F32)],
        name="grads",
        first=SMEM,
    )
    send, kept = small(
        fold_kernel,
        [shape(piece, BF16), shape(piece, F32)],
        (keep, grp_swap(send, 1), *gathered),
        name="fold",
    )
    own, squares = small(
        functools.partial(combine_kernel, (cands // 2, lines, width)),
        [shape((cands, slice_width), BF16), shape((cands, 128), F32)],
        (kept, grp_swap(send, 2)),
        [pltpu.VMEM(piece, F32)],
        name="combine",
    )
    place = pltpu.VMEM((far, cands, nq), F32)
    back = small(
        functools.partial(other_kernel, far),
        shape((cands, total_q // 2), F32),
        (blk_swap(own, 1), *gathered),
        [place],
        name="other_scores",
    )
    line = (owned, total_q + 128)
    send, keep = small(
        functools.partial(own_kernel, (far, groups)),
        [shape((groups // 2,) + line, F32)] * 2,
        (own, squares, *gathered, blk_swap(back, 1)),
        [place, pltpu.VMEM((groups,) + line, F32)],
        name="own_scores",
    )
    send, kept = small(pass_kernel, [shape(line, F32)] * 2, (keep, grp_swap(send, 2)), name="pass")
    return small(
        functools.partial(finish_kernel, (pdim, nq)),
        shape((owned, total_q), F32),
        (kept, grp_swap(send, 1)),
        name="finish",
    )


def solution(mesh):
    in_specs = (
        P(None, "blk", "grp", None),
        P(None, "blk", "grp", None),
        P(),
        P(),
        P("blk"),
        P("blk", None),
    )
    return jax.shard_map(
        functools.partial(on_device, mesh.shape["blk"], mesh.shape["grp"]),
        mesh=mesh,
        in_specs=in_specs,
        out_specs=P(("blk", "grp"), None),
        check_vma=False,
    )
```

```python
import functools

import jax
import jax.numpy as jnp
from jax import lax
from jax.experimental import pallas as pl
from jax.experimental.pallas import tpu as pltpu
from jax.sharding import PartitionSpec as P

EPS = 1e-06
F32 = jnp.float32
BF16 = jnp.bfloat16
VMEM = pl.BlockSpec(memory_space=pltpu.VMEM)
SMEM = pl.BlockSpec(memory_space=pltpu.SMEM)
BY_ROWS = (((1,), (1,)), ((), ()))


def cut_kernel(queries, out, sem):
    part = out.shape[1]
    column = pl.multiple_of((lax.axis_index("grp") // 2) * part, part)
    load = pltpu.make_async_copy(queries.at[:, pl.ds(column, part)], out, sem)
    load.start()
    load.wait()


def grads_kernel(dims, lens, xp_in, gp_in, send, keep):
    cands, tokens, width, slices = dims
    half = cands // 2
    rows = 4 * tokens
    lines = width // slices
    position = lax.broadcasted_iota(jnp.int32, (tokens, width), 0) + lax.axis_index("grp") * tokens
    row_blk = lax.broadcasted_iota(jnp.int32, (rows, rows), 0) // tokens
    col_blk = lax.broadcasted_iota(jnp.int32, (rows, 4 * width), 1) // width
    diagonal = row_blk == col_blk // 2 + 2 * (col_blk % 2)
    for i in range(half // 2):
        members = [2 * i, 2 * i + 1, 2 * i + half, 2 * i + 1 + half]
        parts = [slice(cand * tokens, (cand + 2) * tokens) for cand in members[::2]]
        left = jnp.concatenate([gp_in[:, part] for part in parts], axis=1)
        xp = jnp.concatenate([xp_in[:, part].astype(F32).T for part in parts], axis=0)
        used = [
            jnp.where(position < lens[cand], xp[j * tokens : (j + 1) * tokens], 0.0)
            for j, cand in enumerate(members)
        ]
        wide = jnp.concatenate([jnp.concatenate(used, axis=0)] * 4, axis=1)
        right = jnp.where(diagonal, wide, 0.0).astype(BF16)
        blocks = jnp.dot(left, right, preferred_element_type=F32)
        for t in range(2):
            here = slice((2 * i + t) * lines, (2 * i + t + 1) * lines)
            for s in range(slices):
                block = blocks[s * lines : (s + 1) * lines, t * 128 : (t + 1) * 128]
                keep[s, here, :] = block
                send[s, here, :] = block.astype(BF16)


def fold_kernel(keep, came, *rest):
    send, kept = rest[-2:]
    x = lax.axis_index("grp") // 2
    send[...] = (keep[1 - x] + came[1 - x].astype(F32)).astype(BF16)
    kept[...] = keep[x] + came[x].astype(F32)


def combine_kernel(dims, kept, came, out, squares, grads):
    half, lines, width = dims
    grads[...] = kept[...] + came[...].astype(F32)
    low = lax.broadcasted_iota(jnp.int32, (half, 128), 1) < width
    sums, columns = None, []
    for e in range(0, lines, 2):
        first = grads[pl.ds(e, half, stride=lines), :]
        second = grads[pl.ds(e + 1, half, stride=lines), :]
        line = jnp.concatenate(
            [
                jnp.where(low, first, pltpu.roll(second, width, 1)),
                jnp.where(low, pltpu.roll(first, width, 1), second),
            ],
            axis=0,
        )
        columns.append(line.astype(BF16))
        sums = line * line if sums is None else sums + line * line
    squares[...] = sums
    out[...] = jnp.concatenate(columns, axis=1)


def near_scores(left, queries, place):
    far = len(queries)
    z = lax.axis_index("blk") // 2
    for k in range(far):
        place[jnp.bitwise_xor(z, k)] = lax.dot_general(
            left, queries[k][...], BY_ROWS, preferred_element_type=F32
        )
    return jnp.concatenate([place[k] for k in range(far)], axis=1)


def other_kernel(far, left, *refs):
    refs[far][...] = near_scores(left[...], refs[:far], refs[far + 1])


def own_kernel(dims, left, squares, *refs):
    far, slices = dims
    queries = refs[:far]
    other, send, keep, place, result = refs[far:]
    own = near_scores(left[...], queries, place)
    is_even = lax.rem(lax.axis_index("blk"), 2) == 0
    back = other[...]
    even = jnp.where(is_even, own, back)
    odd = jnp.where(is_even, back, own)
    half = own.shape[1]
    owned = own.shape[0] // slices
    for s in range(slices):
        here = slice(s * owned, (s + 1) * owned)
        result[s, :, :half] = even[here]
        result[s, :, half : 2 * half] = odd[here]
        result[s, :, 2 * half :] = squares[here, :]
    x = lax.axis_index("grp") // 2
    send[...] = result[1 - x]
    keep[...] = result[x]


def scale_kernel(dims, kept, came, first, second):
    pdim, nq = dims
    total = kept[...] + came[...]
    width = first.shape[1]
    mean = jnp.sum(total[:, width:], axis=1, keepdims=True) / pdim
    scaled = total[:, :width] * lax.rsqrt(mean + EPS)
    columns = []
    for start in range(0, width // 2, nq):
        columns.append(scaled[:, start : start + nq])
        columns.append(scaled[:, width // 2 + start : width // 2 + start + nq])
    rows = jnp.concatenate(columns, axis=1)
    owned = first.shape[0]
    first[...] = rows[:owned]
    second[...] = rows[owned:]


def small(kernel, out_shape, operands, scratch_shapes=(), name=None, first=VMEM):
    one = not isinstance(out_shape, list)
    return pl.pallas_call(
        kernel,
        out_shape=out_shape,
        in_specs=[first] + [VMEM] * (len(operands) - 1),
        out_specs=VMEM if one else [VMEM] * len(out_shape),
        scratch_shapes=list(scratch_shapes),
        compiler_params=pltpu.CompilerParams(vmem_limit_bytes=16 * 2**20),
        name=name,
    )(*operands)


def on_device(blks, groups, acts, out_grads, proj_in, proj_out, lengths, queries):
    _, cands, tokens, depth = acts.shape
    width = proj_in.shape[2]
    far = blks // 2
    slices = groups // 2
    pdim = width * width
    lines = width // slices
    nq = queries.shape[0]
    total_q = nq * blks
    owned = cands // groups
    slice_width = pdim // slices
    shape = jax.ShapeDtypeStruct

    def lead_swap(x, blk_flip, grp_flip):
        pairs = [
            (b * groups + g, (b ^ blk_flip) * groups + (g ^ grp_flip))
            for b in range(blks)
            for g in range(1, groups, 2)
        ]
        return lax.ppermute(x, ("blk", "grp"), pairs)

    cut = pl.pallas_call(
        cut_kernel,
        out_shape=shape((nq, slice_width), BF16),
        in_specs=[pl.BlockSpec(memory_space=pl.ANY)],
        out_specs=VMEM,
        scratch_shapes=[pltpu.SemaphoreType.DMA],
        compiler_params=pltpu.CompilerParams(vmem_limit_bytes=4 * 2**20),
        cost_estimate=pl.CostEstimate(flops=0, bytes_accessed=64 * 2**20, transcendentals=0),
        name="cut",
    )(queries)
    gathered = [cut] + [lead_swap(cut, 2 * k, 0) for k in range(1, far)]

    rows = cands * tokens
    piece = (cands // 2 * lines, 128)
    gp = jnp.dot(out_grads.reshape(rows, depth), proj_out[0], preferred_element_type=F32).astype(BF16)
    xp = jnp.dot(acts.reshape(rows, depth), proj_in[0], preferred_element_type=F32).astype(BF16)
    send, keep = small(
        functools.partial(grads_kernel, (cands, tokens, width, slices)),
        [shape((slices,) + piece, BF16), shape((slices,) + piece, F32)],
        (lengths, xp.T, gp.T),
        name="grads",
        first=SMEM,
    )
    came = lax.ppermute(send, "grp", [(g, g + 1) for g in range(0, groups, 2)])
    send, kept = small(
        fold_kernel, [shape(piece, BF16), shape(piece, F32)], (keep, came, *gathered), name="fold"
    )
    own, squares = small(
        functools.partial(combine_kernel, (cands // 2, lines, width)),
        [shape((cands, slice_width), BF16), shape((cands, 128), F32)],
        (kept, lead_swap(send, 0, 2)),
        [pltpu.VMEM(piece, F32)],
        name="combine",
    )
    place = pltpu.VMEM((far, cands, nq), F32)
    back = small(
        functools.partial(other_kernel, far),
        shape((cands, total_q // 2), F32),
        (lead_swap(own, 1, 0), *gathered),
        [place],
        name="other_scores",
    )
    line = (cands // slices, total_q + 128)
    send, keep = small(
        functools.partial(own_kernel, (far, slices)),
        [shape(line, F32)] * 2,
        (own, squares, *gathered, lead_swap(back, 1, 0)),
        [place, pltpu.VMEM((slices,) + line, F32)],
        name="own_scores",
    )
    first, second = small(
        functools.partial(scale_kernel, (pdim, nq)),
        [shape((owned, total_q), F32)] * 2,
        (keep, lead_swap(send, 0, 2)),
        name="scale",
    )
    came = lax.ppermute(first, "grp", [(g + 1, g) for g in range(0, groups, 2)])
    return jnp.where(lax.rem(lax.axis_index("grp"), 2) == 0, came, second)


def solution(mesh):
    in_specs = (
        P(None, "blk", "grp", None),
        P(None, "blk", "grp", None),
        P(),
        P(),
        P("blk"),
        P("blk", None),
    )
    return jax.shard_map(
        functools.partial(on_device, mesh.shape["blk"], mesh.shape["grp"]),
        mesh=mesh,
        in_specs=in_specs,
        out_specs=P(("blk", "grp"), None),
        check_vma=False,
    )
```

```python
import functools

import jax
import jax.numpy as jnp
from jax import lax
from jax.experimental import pallas as pl
from jax.experimental.pallas import tpu as pltpu
from jax.sharding import PartitionSpec as P

EPS = 1e-06
GRANT = 54784
F32 = jnp.float32
BF16 = jnp.bfloat16
VMEM = pl.BlockSpec(memory_space=pltpu.VMEM)
ANY = pl.BlockSpec(memory_space=pl.ANY)
BY_ROWS = (((1,), (1,)), ((), ()))


def cut_kernel(queries, out, sem):
    part = out.shape[1]
    column = pl.multiple_of((lax.axis_index("grp") // 2) * part, part)
    load = pltpu.make_async_copy(queries.at[:, pl.ds(column, part)], out, sem)
    load.start()
    load.wait()


def grads_kernel(dims, lens_in, acts, grads, w_in, w_out, send, keep, *scratch):
    cands, tokens, width, slices = dims
    act_buf, grad_buf, win_raw, wout_raw, win, wout, lens, sems, wsems = scratch
    half = cands // 2
    chunks = half // 2
    rows = 4 * tokens
    loads = []
    for i in range(chunks):
        for side, (source, buf) in enumerate(((grads, grad_buf), (acts, act_buf))):
            loads.append(
                [
                    pltpu.make_async_copy(
                        source.at[pl.ds((2 * i + h * half) * tokens, rows // 2)],
                        buf.at[pl.ds(i * rows + h * (rows // 2), rows // 2)],
                        sems.at[side, 2 * i + h],
                    )
                    for h in range(2)
                ]
            )

    def start(n):
        if n < len(loads):
            for load in loads[n]:
                load.start()

    def wait(n):
        for load in loads[n]:
            load.wait()

    load_lens = pltpu.make_async_copy(lens_in, lens, wsems.at[2])
    load_wout = pltpu.make_async_copy(w_out, wout_raw, wsems.at[0])
    load_win = pltpu.make_async_copy(w_in, win_raw, wsems.at[1])
    load_wout.start()
    load_win.start()
    load_lens.start()
    start(0)
    start(1)
    lines = width // slices
    position = lax.broadcasted_iota(jnp.int32, (tokens, width), 0) + lax.axis_index("grp") * tokens
    row_blk = lax.broadcasted_iota(jnp.int32, (rows, rows), 0) // tokens
    col_blk = lax.broadcasted_iota(jnp.int32, (rows, 4 * width), 1) // width
    diagonal = row_blk == col_blk // 2 + 2 * (col_blk % 2)
    load_wout.wait()
    wout[...] = wout_raw[...].T
    load_win.wait()
    win[...] = win_raw[...].T
    load_lens.wait()
    for i in range(chunks):
        part = pl.ds(i * rows, rows)
        wait(2 * i)
        start(2 * i + 2)
        gp = jnp.dot(grad_buf[part, :], wout[...], preferred_element_type=F32)
        left = gp.T.astype(BF16)
        wait(2 * i + 1)
        start(2 * i + 3)
        xp = jnp.dot(act_buf[part, :], win[...], preferred_element_type=F32)
        used = []
        for j in range(4):
            cand = 2 * i + j % 2 + (j // 2) * half
            used.append(jnp.where(position < lens[cand], xp[j * tokens : (j + 1) * tokens], 0.0))
        wide = jnp.concatenate([jnp.concatenate(used, axis=0)] * 4, axis=1)
        right = jnp.where(diagonal, wide, 0.0).astype(BF16)
        sums = jnp.dot(left, right, preferred_element_type=F32)
        for t in range(2):
            there = slice((2 * i + t) * lines, (2 * i + t + 1) * lines)
            for s in range(slices):
                block = sums[s * lines : (s + 1) * lines, t * 128 : (t + 1) * 128]
                keep[s, there, :] = block
                send[s, there, :] = block.astype(BF16)


def fold_kernel(keep, came, *rest):
    send, kept = rest[-2:]
    x = lax.axis_index("grp") // 2
    send[...] = (keep[1 - x] + came[1 - x].astype(F32)).astype(BF16)
    kept[...] = keep[x] + came[x].astype(F32)


def combine_kernel(dims, kept, came, out, squares, grads):
    half, lines, width = dims
    grads[...] = kept[...] + came[...].astype(F32)
    low = lax.broadcasted_iota(jnp.int32, (half, 128), 1) < width
    sums, columns = None, []
    for e in range(0, lines, 2):
        first = grads[pl.ds(e, half, stride=lines), :]
        second = grads[pl.ds(e + 1, half, stride=lines), :]
        line = jnp.concatenate(
            [
                jnp.where(low, first, pltpu.roll(second, width, 1)),
                jnp.where(low, pltpu.roll(first, width, 1), second),
            ],
            axis=0,
        )
        columns.append(line.astype(BF16))
        sums = line * line if sums is None else sums + line * line
    squares[...] = sums
    out[...] = jnp.concatenate(columns, axis=1)


def near_scores(left, queries, place):
    far = len(queries)
    z = lax.axis_index("blk") // 2
    for k in range(far):
        place[jnp.bitwise_xor(z, k)] = lax.dot_general(
            left, queries[k][...], BY_ROWS, preferred_element_type=F32
        )
    return jnp.concatenate([place[k] for k in range(far)], axis=1)


def other_kernel(far, left, *refs):
    refs[far][...] = near_scores(left[...], refs[:far], refs[far + 1])


def own_kernel(dims, left, squares, *refs):
    far, slices = dims
    queries = refs[:far]
    other, send, keep, place, result = refs[far:]
    own = near_scores(left[...], queries, place)
    is_even = lax.rem(lax.axis_index("blk"), 2) == 0
    back = other[...]
    even = jnp.where(is_even, own, back)
    odd = jnp.where(is_even, back, own)
    half = own.shape[1]
    owned = own.shape[0] // slices
    for s in range(slices):
        here = slice(s * owned, (s + 1) * owned)
        result[s, :, :half] = even[here]
        result[s, :, half : 2 * half] = odd[here]
        result[s, :, 2 * half :] = squares[here, :]
    x = lax.axis_index("grp") // 2
    send[...] = result[1 - x]
    keep[...] = result[x]


def scale_kernel(dims, kept, came, first, second):
    pdim, nq = dims
    total = kept[...] + came[...]
    width = first.shape[1]
    mean = jnp.sum(total[:, width:], axis=1, keepdims=True) / pdim
    scaled = total[:, :width] * lax.rsqrt(mean + EPS)
    columns = []
    for start in range(0, width // 2, nq):
        columns.append(scaled[:, start : start + nq])
        columns.append(scaled[:, width // 2 + start : width // 2 + start + nq])
    rows = jnp.concatenate(columns, axis=1)
    owned = first.shape[0]
    first[...] = rows[:owned]
    second[...] = rows[owned:]


def small(kernel, out_shape, operands, scratch_shapes=(), name=None):
    one = not isinstance(out_shape, list)
    return pl.pallas_call(
        kernel,
        out_shape=out_shape,
        in_specs=[VMEM] * len(operands),
        out_specs=VMEM if one else [VMEM] * len(out_shape),
        scratch_shapes=list(scratch_shapes),
        compiler_params=pltpu.CompilerParams(vmem_limit_bytes=16 * 2**20),
        name=name,
    )(*operands)


def on_device(blks, groups, acts, out_grads, proj_in, proj_out, lengths, queries):
    _, cands, tokens, depth = acts.shape
    width = proj_in.shape[2]
    far = blks // 2
    slices = groups // 2
    pdim = width * width
    lines = width // slices
    nq = queries.shape[0]
    total_q = nq * blks
    owned = cands // groups
    slice_width = pdim // slices
    shape = jax.ShapeDtypeStruct

    def lead_swap(x, blk_flip, grp_flip):
        pairs = [
            (b * groups + g, (b ^ blk_flip) * groups + (g ^ grp_flip) if g % 2 else b * groups + g)
            for b in range(blks)
            for g in range(groups)
        ]
        return lax.ppermute(x, ("blk", "grp"), pairs)

    cut = pl.pallas_call(
        cut_kernel,
        out_shape=shape((nq, slice_width), BF16),
        in_specs=[ANY],
        out_specs=VMEM,
        scratch_shapes=[pltpu.SemaphoreType.DMA],
        compiler_params=pltpu.CompilerParams(vmem_limit_bytes=4 * 2**20),
        cost_estimate=pl.CostEstimate(flops=0, bytes_accessed=2 * nq * slice_width * 2, transcendentals=0),
        name="cut",
    )(queries)
    gathered = [cut] + [lead_swap(cut, 2 * k, 0) for k in range(1, far)]

    rows = cands * tokens
    piece = (cands // 2 * lines, 128)
    send, keep = pl.pallas_call(
        functools.partial(grads_kernel, (cands, tokens, width, slices)),
        out_shape=[shape((slices,) + piece, BF16), shape((slices,) + piece, F32)],
        in_specs=[ANY] * 5,
        out_specs=[VMEM] * 2,
        scratch_shapes=[
            pltpu.VMEM((rows, depth), BF16),
            pltpu.VMEM((rows, depth), BF16),
            pltpu.VMEM((width, depth), BF16),
            pltpu.VMEM((width, depth), BF16),
            pltpu.VMEM((depth, width), BF16),
            pltpu.VMEM((depth, width), BF16),
            pltpu.SMEM((cands,), jnp.int32),
            pltpu.SemaphoreType.DMA((2, cands // 2)),
            pltpu.SemaphoreType.DMA((3,)),
        ],
        compiler_params=pltpu.CompilerParams(vmem_limit_bytes=GRANT * 2**10),
        cost_estimate=pl.CostEstimate(
            flops=16 * rows * depth * width, bytes_accessed=4 * rows * depth, transcendentals=0
        ),
        name="grads",
    )(
        lengths,
        acts.reshape(rows, depth),
        out_grads.reshape(rows, depth),
        proj_in[0].T,
        proj_out[0].T,
    )
    came = lax.ppermute(send, "grp", [(g, g ^ 1) for g in range(groups)])
    send, kept = small(
        fold_kernel, [shape(piece, BF16), shape(piece, F32)], (keep, came, *gathered), name="fold"
    )
    own, squares = small(
        functools.partial(combine_kernel, (cands // 2, lines, width)),
        [shape((cands, slice_width), BF16), shape((cands, 128), F32)],
        (kept, lead_swap(send, 0, 2)),
        [pltpu.VMEM(piece, F32)],
        name="combine",
    )
    place = pltpu.VMEM((far, cands, nq), F32)
    back = small(
        functools.partial(other_kernel, far),
        shape((cands, total_q // 2), F32),
        (lead_swap(own, 1, 0), *gathered),
        [place],
        name="other_scores",
    )
    line = (cands // slices, total_q + 128)
    send, keep = small(
        functools.partial(own_kernel, (far, slices)),
        [shape(line, F32)] * 2,
        (own, squares, *gathered, lead_swap(back, 1, 0)),
        [place, pltpu.VMEM((slices,) + line, F32)],
        name="own_scores",
    )
    first, second = small(
        functools.partial(scale_kernel, (pdim, nq)),
        [shape((owned, total_q), F32)] * 2,
        (keep, lead_swap(send, 0, 2)),
        name="scale",
    )
    came = lax.ppermute(first, "grp", [(g, g ^ 1) for g in range(groups)])
    return jnp.where(lax.rem(lax.axis_index("grp"), 2) == 0, came, second)


def solution(mesh):
    in_specs = (
        P(None, "blk", "grp", None),
        P(None, "blk", "grp", None),
        P(),
        P(),
        P("blk"),
        P("blk", None),
    )
    return jax.shard_map(
        functools.partial(on_device, mesh.shape["blk"], mesh.shape["grp"]),
        mesh=mesh,
        in_specs=in_specs,
        out_specs=P(("blk", "grp"), None),
        check_vma=False,
    )
```

```python
import functools

import jax
import jax.numpy as jnp
from jax import lax
from jax.experimental import pallas as pl
from jax.experimental.pallas import tpu as pltpu
from jax.sharding import PartitionSpec as P

EPS = 1e-06
F32 = jnp.float32
BF16 = jnp.bfloat16
VMEM = pl.BlockSpec(memory_space=pltpu.VMEM)
SMEM = pl.BlockSpec(memory_space=pltpu.SMEM)
BY_ROWS = (((1,), (1,)), ((), ()))


def grads_kernel(dims, lens, xp_in, gp_in, send, keep, store):
    cands, tokens, width, groups = dims
    half = cands // 2
    rows = 4 * tokens
    grp = lax.axis_index("grp")
    lines = width // groups
    position = lax.broadcasted_iota(jnp.int32, (tokens, width), 0) + grp * tokens
    row_blk = lax.broadcasted_iota(jnp.int32, (rows, rows), 0) // tokens
    col_blk = lax.broadcasted_iota(jnp.int32, (rows, 4 * width), 1) // width
    diagonal = row_blk == col_blk // 2 + 2 * (col_blk % 2)
    for i in range(half // 2):
        members = [2 * i, 2 * i + 1, 2 * i + half, 2 * i + 1 + half]
        parts = [slice(cand * tokens, (cand + 2) * tokens) for cand in members[::2]]
        left = jnp.concatenate([gp_in[:, part] for part in parts], axis=1)
        xp = jnp.concatenate([xp_in[:, part].astype(F32).T for part in parts], axis=0)
        used = [
            jnp.where(position < lens[cand], xp[j * tokens : (j + 1) * tokens], 0.0)
            for j, cand in enumerate(members)
        ]
        wide = jnp.concatenate([jnp.concatenate(used, axis=0)] * 4, axis=1)
        right = jnp.where(diagonal, wide, 0.0).astype(BF16)
        blocks = jnp.dot(left, right, preferred_element_type=F32)
        for t in range(2):
            pair = 2 * i + t
            for s in range(groups):
                store[s, pair * lines : (pair + 1) * lines, :] = blocks[
                    s * lines : (s + 1) * lines, t * 128 : (t + 1) * 128
                ]
    core = lax.rem(grp, 2)
    for x in range(groups // 2):
        send[x] = store[2 * x + 1 - core].astype(BF16)
        keep[x] = store[2 * x + core]


def fold_kernel(keep, came, *rest):
    send, kept = rest[-2:]
    x = lax.axis_index("grp") // 2
    send[...] = (keep[1 - x] + came[1 - x].astype(F32)).astype(BF16)
    kept[...] = keep[x] + came[x].astype(F32)


def combine_kernel(dims, kept, came, *rest):
    half, lines, width = dims
    out, squares, grads = rest[-3:]
    grads[...] = kept[...] + came[...].astype(F32)
    low = lax.broadcasted_iota(jnp.int32, (half, 128), 1) < width
    sums, columns = None, []
    for e in range(0, lines, 2):
        first = grads[pl.ds(e, half, stride=lines), :]
        second = grads[pl.ds(e + 1, half, stride=lines), :]
        line = jnp.concatenate(
            [
                jnp.where(low, first, pltpu.roll(second, width, 1)),
                jnp.where(low, pltpu.roll(first, width, 1), second),
            ],
            axis=0,
        )
        columns.append(line.astype(BF16))
        sums = line * line if sums is None else sums + line * line
    squares[...] = sums
    out[...] = jnp.concatenate(columns, axis=1)


def join_kernel(count, *refs):
    out = refs[-1]
    nq = refs[-2].shape[0]
    for n, ref in enumerate(refs[-1 - count : -1]):
        out[n * nq : (n + 1) * nq, :] = ref[...]


def scores_kernel(dims, left, squares, *refs):
    blks, groups = dims
    pieces = refs[: blks // 2 + 2]
    far, send, keep, place, result = refs[blks // 2 + 2 :]
    rows = left[...]
    blk = lax.axis_index("blk")
    nq = pieces[0].shape[0]
    table = {0: pieces[0], 1: pieces[1], 2: pieces[2], 3: pieces[3]}
    for k in range(2, blks // 2):
        table[2 * k] = pieces[k + 2]
        table[2 * k + 1] = far.at[pl.ds((k - 2) * nq, nq)]
    for flip, piece in table.items():
        place[jnp.bitwise_xor(blk, flip)] = lax.dot_general(
            rows, piece[...], BY_ROWS, preferred_element_type=F32
        )
    scores = jnp.concatenate([place[b] for b in range(blks)], axis=1)
    width = blks * nq
    owned = scores.shape[0] // groups
    for g in range(groups):
        here = slice(g * owned, (g + 1) * owned)
        result[g, :, :width] = scores[here]
        result[g, :, width:] = squares[here, :]
    x = lax.axis_index("grp") // 2
    for core in range(2):
        send[core] = result[2 * (1 - x) + core]
        keep[core] = result[2 * x + core]


def pass_kernel(keep, came, send, kept):
    core = lax.rem(lax.axis_index("grp"), 2)
    send[...] = keep[1 - core] + came[1 - core]
    kept[...] = keep[core] + came[core]


def finish_kernel(pdim, kept, came, out):
    total = kept[...] + came[...]
    width = out.shape[1]
    mean = jnp.sum(total[:, width:], axis=1, keepdims=True) / pdim
    out[...] = total[:, :width] * lax.rsqrt(mean + EPS)


def small(kernel, out_shape, operands, scratch_shapes=(), name=None, first=VMEM):
    one = not isinstance(out_shape, list)
    return pl.pallas_call(
        kernel,
        out_shape=out_shape,
        in_specs=[first] + [VMEM] * (len(operands) - 1),
        out_specs=VMEM if one else [VMEM] * len(out_shape),
        scratch_shapes=list(scratch_shapes),
        compiler_params=pltpu.CompilerParams(vmem_limit_bytes=16 * 2**20),
        name=name,
    )(*operands)


def on_device(blks, groups, acts, out_grads, proj_in, proj_out, lengths, queries):
    _, cands, tokens, depth = acts.shape
    width = proj_in.shape[2]
    far = blks // 2
    pdim = width * width
    lines = width // groups
    nq = queries.shape[0]
    total_q = nq * blks
    owned = cands // groups
    slice_width = pdim // groups
    shape = jax.ShapeDtypeStruct

    def grp_swap(x, k):
        return lax.ppermute(x, "grp", [(g, g ^ k) for g in range(groups)])

    def blk_swap(x, k):
        return lax.ppermute(x, "blk", [(b, b ^ k) for b in range(blks)])

    cut = lax.dynamic_slice(queries, (0, lax.axis_index("grp") * slice_width), (nq, slice_width))
    pieces = [cut, blk_swap(cut, 1), blk_swap(cut, 2), blk_swap(cut, 3)]
    distant = [blk_swap(cut, 2 * k) for k in range(2, far)]

    rows = cands * tokens
    piece = (cands // 2 * lines, 128)
    gp = jnp.dot(out_grads.reshape(rows, depth), proj_out[0], preferred_element_type=F32).astype(BF16)
    xp = jnp.dot(acts.reshape(rows, depth), proj_in[0], preferred_element_type=F32).astype(BF16)
    send, keep = small(
        functools.partial(grads_kernel, (cands, tokens, width, groups)),
        [shape((groups // 2,) + piece, BF16), shape((groups // 2,) + piece, F32)],
        (lengths, xp.T, gp.T),
        [pltpu.VMEM((groups,) + piece, F32)],
        name="grads",
        first=SMEM,
    )
    joined = small(
        functools.partial(join_kernel, far - 2),
        shape(((far - 2) * nq, slice_width), BF16),
        (*pieces[1:], keep, *distant),
        name="join",
    )
    send, kept = small(
        fold_kernel,
        [shape(piece, BF16), shape(piece, F32)],
        (keep, grp_swap(send, 1), joined),
        name="fold",
    )
    passed = blk_swap(joined, 1)
    own, squares = small(
        functools.partial(combine_kernel, (cands // 2, lines, width)),
        [shape((cands, slice_width), BF16), shape((cands, 128), F32)],
        (kept, grp_swap(send, 2), passed),
        [pltpu.VMEM(piece, F32)],
        name="combine",
    )
    line = (owned, total_q + 128)
    send, keep = small(
        functools.partial(scores_kernel, (blks, groups)),
        [shape((groups // 2,) + line, F32)] * 2,
        (own, squares, *pieces, *distant, passed),
        [pltpu.VMEM((blks, cands, nq), F32), pltpu.VMEM((groups,) + line, F32)],
        name="scores",
    )
    send, kept = small(pass_kernel, [shape(line, F32)] * 2, (keep, grp_swap(send, 2)), name="pass")
    return small(
        functools.partial(finish_kernel, pdim),
        shape((owned, total_q), F32),
        (kept, grp_swap(send, 1)),
        name="finish",
    )


def solution(mesh):
    in_specs = (
        P(None, "blk", "grp", None),
        P(None, "blk", "grp", None),
        P(),
        P(),
        P("blk"),
        P("blk", None),
    )
    return jax.shard_map(
        functools.partial(on_device, mesh.shape["blk"], mesh.shape["grp"]),
        mesh=mesh,
        in_specs=in_specs,
        out_specs=P(("blk", "grp"), None),
        check_vma=False,
    )
```

```python
import functools

import jax
import jax.numpy as jnp
from jax import lax
from jax.experimental import pallas as pl
from jax.experimental.pallas import tpu as pltpu
from jax.sharding import PartitionSpec as P

EPS = 1e-06
GRANT = 54784
F32 = jnp.float32
BF16 = jnp.bfloat16
VMEM = pl.BlockSpec(memory_space=pltpu.VMEM)
ANY = pl.BlockSpec(memory_space=pl.ANY)
BY_ROWS = (((1,), (1,)), ((), ()))


def grads_kernel(dims, lens_in, acts, grads, w_in, w_out, send, keep, *scratch):
    cands, tokens, width, groups = dims
    act_buf, grad_buf, win_raw, wout_raw, win, wout, lens, store, sems, wsems = scratch
    half = cands // 2
    chunks = half // 2
    rows = 4 * tokens
    loads = []
    for i in range(chunks):
        for side, (source, buf) in enumerate(((grads, grad_buf), (acts, act_buf))):
            loads.append(
                [
                    pltpu.make_async_copy(
                        source.at[pl.ds((2 * i + h * half) * tokens, rows // 2)],
                        buf.at[pl.ds(i * rows + h * (rows // 2), rows // 2)],
                        sems.at[side, 2 * i + h],
                    )
                    for h in range(2)
                ]
            )

    def start(n):
        if n < len(loads):
            for load in loads[n]:
                load.start()

    def wait(n):
        for load in loads[n]:
            load.wait()

    load_lens = pltpu.make_async_copy(lens_in, lens, wsems.at[2])
    load_wout = pltpu.make_async_copy(w_out, wout_raw, wsems.at[0])
    load_win = pltpu.make_async_copy(w_in, win_raw, wsems.at[1])
    load_wout.start()
    start(0)
    load_win.start()
    load_lens.start()
    grp = lax.axis_index("grp")
    lines = width // groups
    position = lax.broadcasted_iota(jnp.int32, (tokens, width), 0) + grp * tokens
    row_blk = lax.broadcasted_iota(jnp.int32, (rows, rows), 0) // tokens
    col_blk = lax.broadcasted_iota(jnp.int32, (rows, 4 * width), 1) // width
    diagonal = row_blk == col_blk // 2 + 2 * (col_blk % 2)

    def add_up(i, left, xp):
        used = []
        for j in range(4):
            cand = 2 * i + j % 2 + (j // 2) * half
            used.append(jnp.where(position < lens[cand], xp[j * tokens : (j + 1) * tokens], 0.0))
        wide = jnp.concatenate([jnp.concatenate(used, axis=0)] * 4, axis=1)
        right = jnp.where(diagonal, wide, 0.0).astype(BF16)
        sums = jnp.dot(left, right, preferred_element_type=F32)
        for t in range(2):
            there = slice((2 * i + t) * lines, (2 * i + t + 1) * lines)
            for s in range(groups):
                store[s, there, :] = sums[s * lines : (s + 1) * lines, t * 128 : (t + 1) * 128]

    load_wout.wait()
    start(1)
    wout[...] = wout_raw[...].T
    load_win.wait()
    load_lens.wait()
    pending = None
    for i in range(chunks):
        part = pl.ds(i * rows, rows)
        wait(2 * i)
        start(2 * i + 2)
        gp = jnp.dot(grad_buf[part, :], wout[...], preferred_element_type=F32)
        if i == 0:
            win[...] = win_raw[...].T
        else:
            add_up(*pending)
        left = gp.T.astype(BF16)
        wait(2 * i + 1)
        start(2 * i + 3)
        xp = jnp.dot(act_buf[part, :], win[...], preferred_element_type=F32)
        pending = (i, left, xp)
    add_up(*pending)
    core = lax.rem(grp, 2)
    for x in range(groups // 2):
        send[x] = store[2 * x + 1 - core].astype(BF16)
        keep[x] = store[2 * x + core]


def fold_kernel(keep, came, *rest):
    send, kept = rest[-2:]
    x = lax.axis_index("grp") // 2
    send[...] = (keep[1 - x] + came[1 - x].astype(F32)).astype(BF16)
    kept[...] = keep[x] + came[x].astype(F32)


def combine_kernel(dims, kept, came, *rest):
    half, lines, width = dims
    out, squares, grads = rest[-3:]
    grads[...] = kept[...] + came[...].astype(F32)
    low = lax.broadcasted_iota(jnp.int32, (half, 128), 1) < width
    sums, columns = None, []
    for e in range(0, lines, 2):
        first = grads[pl.ds(e, half, stride=lines), :]
        second = grads[pl.ds(e + 1, half, stride=lines), :]
        line = jnp.concatenate(
            [
                jnp.where(low, first, pltpu.roll(second, width, 1)),
                jnp.where(low, pltpu.roll(first, width, 1), second),
            ],
            axis=0,
        )
        columns.append(line.astype(BF16))
        sums = line * line if sums is None else sums + line * line
    squares[...] = sums
    out[...] = jnp.concatenate(columns, axis=1)


def join_kernel(count, *refs):
    out = refs[-1]
    nq = refs[-2].shape[0]
    for n, ref in enumerate(refs[-1 - count : -1]):
        out[n * nq : (n + 1) * nq, :] = ref[...]


def scores_kernel(dims, left, squares, *refs):
    blks, groups = dims
    pieces = refs[: blks // 2 + 2]
    far, send, keep, place, result = refs[blks // 2 + 2 :]
    rows = left[...]
    blk = lax.axis_index("blk")
    nq = pieces[0].shape[0]
    table = {0: pieces[0], 1: pieces[1], 2: pieces[2], 3: pieces[3]}
    for k in range(2, blks // 2):
        table[2 * k] = pieces[k + 2]
        table[2 * k + 1] = far.at[pl.ds((k - 2) * nq, nq)]
    for flip, piece in table.items():
        place[jnp.bitwise_xor(blk, flip)] = lax.dot_general(
            rows, piece[...], BY_ROWS, preferred_element_type=F32
        )
    scores = jnp.concatenate([place[b] for b in range(blks)], axis=1)
    width = blks * nq
    owned = scores.shape[0] // groups
    for g in range(groups):
        here = slice(g * owned, (g + 1) * owned)
        result[g, :, :width] = scores[here]
        result[g, :, width:] = squares[here, :]
    x = lax.axis_index("grp") // 2
    for core in range(2):
        send[core] = result[2 * (1 - x) + core]
        keep[core] = result[2 * x + core]


def pass_kernel(keep, came, send, kept):
    core = lax.rem(lax.axis_index("grp"), 2)
    send[...] = keep[1 - core] + came[1 - core]
    kept[...] = keep[core] + came[core]


def finish_kernel(pdim, kept, came, out):
    total = kept[...] + came[...]
    width = out.shape[1]
    mean = jnp.sum(total[:, width:], axis=1, keepdims=True) / pdim
    out[...] = total[:, :width] * lax.rsqrt(mean + EPS)


def small(kernel, out_shape, operands, scratch_shapes=(), name=None):
    one = not isinstance(out_shape, list)
    return pl.pallas_call(
        kernel,
        out_shape=out_shape,
        in_specs=[VMEM] * len(operands),
        out_specs=VMEM if one else [VMEM] * len(out_shape),
        scratch_shapes=list(scratch_shapes),
        compiler_params=pltpu.CompilerParams(vmem_limit_bytes=16 * 2**20),
        name=name,
    )(*operands)


def on_device(blks, groups, acts, out_grads, proj_in, proj_out, lengths, queries):
    _, cands, tokens, depth = acts.shape
    width = proj_in.shape[2]
    far = blks // 2
    pdim = width * width
    lines = width // groups
    nq = queries.shape[0]
    total_q = nq * blks
    owned = cands // groups
    slice_width = pdim // groups
    shape = jax.ShapeDtypeStruct

    def grp_swap(x, k):
        return lax.ppermute(x, "grp", [(g, g ^ k) for g in range(groups)])

    def blk_swap(x, k):
        return lax.ppermute(x, "blk", [(b, b ^ k) for b in range(blks)])

    cut = lax.dynamic_slice(queries, (0, lax.axis_index("grp") * slice_width), (nq, slice_width))
    cut, lens = lax.optimization_barrier((cut, jnp.minimum(lengths, tokens * groups)))
    pieces = [cut, blk_swap(cut, 1), blk_swap(cut, 2), blk_swap(cut, 3)]
    distant = [blk_swap(cut, 2 * k) for k in range(2, far)]

    rows = cands * tokens
    piece = (cands // 2 * lines, 128)
    send, keep = pl.pallas_call(
        functools.partial(grads_kernel, (cands, tokens, width, groups)),
        out_shape=[shape((groups // 2,) + piece, BF16), shape((groups // 2,) + piece, F32)],
        in_specs=[ANY] * 5,
        out_specs=[VMEM] * 2,
        scratch_shapes=[
            pltpu.VMEM((rows, depth), BF16),
            pltpu.VMEM((rows, depth), BF16),
            pltpu.VMEM((width, depth), BF16),
            pltpu.VMEM((width, depth), BF16),
            pltpu.VMEM((depth, width), BF16),
            pltpu.VMEM((depth, width), BF16),
            pltpu.SMEM((cands,), jnp.int32),
            pltpu.VMEM((groups,) + piece, F32),
            pltpu.SemaphoreType.DMA((2, cands // 2)),
            pltpu.SemaphoreType.DMA((3,)),
        ],
        compiler_params=pltpu.CompilerParams(vmem_limit_bytes=GRANT * 2**10),
        cost_estimate=pl.CostEstimate(
            flops=16 * rows * depth * width, bytes_accessed=4 * rows * depth, transcendentals=0
        ),
        name="grads",
    )(
        lens,
        acts.reshape(rows, depth),
        out_grads.reshape(rows, depth),
        proj_in[0].T,
        proj_out[0].T,
    )
    joined = small(
        functools.partial(join_kernel, far - 2),
        shape(((far - 2) * nq, slice_width), BF16),
        (*pieces[1:], keep, *distant),
        name="join",
    )
    send, kept = small(
        fold_kernel,
        [shape(piece, BF16), shape(piece, F32)],
        (keep, grp_swap(send, 1), joined),
        name="fold",
    )
    passed = blk_swap(joined, 1)
    own, squares = small(
        functools.partial(combine_kernel, (cands // 2, lines, width)),
        [shape((cands, slice_width), BF16), shape((cands, 128), F32)],
        (kept, grp_swap(send, 2), passed),
        [pltpu.VMEM(piece, F32)],
        name="combine",
    )
    line = (owned, total_q + 128)
    send, keep = small(
        functools.partial(scores_kernel, (blks, groups)),
        [shape((groups // 2,) + line, F32)] * 2,
        (own, squares, *pieces, *distant, passed),
        [pltpu.VMEM((blks, cands, nq), F32), pltpu.VMEM((groups,) + line, F32)],
        name="scores",
    )
    send, kept = small(pass_kernel, [shape(line, F32)] * 2, (keep, grp_swap(send, 2)), name="pass")
    return small(
        functools.partial(finish_kernel, pdim),
        shape((owned, total_q), F32),
        (kept, grp_swap(send, 1)),
        name="finish",
    )


def solution(mesh):
    in_specs = (
        P(None, "blk", "grp", None),
        P(None, "blk", "grp", None),
        P(),
        P(),
        P("blk"),
        P("blk", None),
    )
    return jax.shard_map(
        functools.partial(on_device, mesh.shape["blk"], mesh.shape["grp"]),
        mesh=mesh,
        in_specs=in_specs,
        out_specs=P(("blk", "grp"), None),
        check_vma=False,
    )
```

```python
import functools

import jax
import jax.numpy as jnp
from jax import lax
from jax.experimental import pallas as pl
from jax.experimental.pallas import tpu as pltpu
from jax.sharding import PartitionSpec as P

EPS = 1e-06
GRANT = 54784
F32 = jnp.float32
BF16 = jnp.bfloat16
VMEM = pl.BlockSpec(memory_space=pltpu.VMEM)
ANY = pl.BlockSpec(memory_space=pl.ANY)
BY_ROWS = (((1,), (1,)), ((), ()))


def grads_kernel(dims, lens_in, acts, grads, w_in, w_out, send, keep, *scratch):
    cands, tokens, width, groups = dims
    act_buf, grad_buf, win_raw, wout_raw, win, wout, lens, store, sems, wsems = scratch
    half = cands // 2
    chunks = half // 2
    rows = 4 * tokens
    loads = []
    for i in range(chunks):
        for side, (source, buf) in enumerate(((grads, grad_buf), (acts, act_buf))):
            loads.append(
                [
                    pltpu.make_async_copy(
                        source.at[pl.ds((2 * i + h * half) * tokens, rows // 2)],
                        buf.at[pl.ds(i * rows + h * (rows // 2), rows // 2)],
                        sems.at[side, 2 * i + h],
                    )
                    for h in range(2)
                ]
            )

    def start(n):
        if n < len(loads):
            for load in loads[n]:
                load.start()

    def wait(n):
        for load in loads[n]:
            load.wait()

    load_lens = pltpu.make_async_copy(lens_in, lens, wsems.at[2])
    load_wout = pltpu.make_async_copy(w_out, wout_raw, wsems.at[0])
    load_win = pltpu.make_async_copy(w_in, win_raw, wsems.at[1])
    load_wout.start()
    load_win.start()
    load_lens.start()
    for n in range(3):
        start(n)
    grp = lax.axis_index("grp")
    lines = width // groups
    position = lax.broadcasted_iota(jnp.int32, (tokens, width), 0) + grp * tokens
    row_blk = lax.broadcasted_iota(jnp.int32, (rows, rows), 0) // tokens
    col_blk = lax.broadcasted_iota(jnp.int32, (rows, 4 * width), 1) // width
    diagonal = row_blk == col_blk // 2 + 2 * (col_blk % 2)

    def add_up(i, left, xp):
        used = []
        for j in range(4):
            cand = 2 * i + j % 2 + (j // 2) * half
            used.append(jnp.where(position < lens[cand], xp[j * tokens : (j + 1) * tokens], 0.0))
        wide = jnp.concatenate([jnp.concatenate(used, axis=0)] * 4, axis=1)
        right = jnp.where(diagonal, wide, 0.0).astype(BF16)
        sums = jnp.dot(left, right, preferred_element_type=F32)
        for t in range(2):
            there = slice((2 * i + t) * lines, (2 * i + t + 1) * lines)
            for s in range(groups):
                store[s, there, :] = sums[s * lines : (s + 1) * lines, t * 128 : (t + 1) * 128]

    load_wout.wait()
    wout[...] = wout_raw[...].T
    load_win.wait()
    load_lens.wait()
    pending = None
    for i in range(chunks):
        part = pl.ds(i * rows, rows)
        wait(2 * i)
        start(2 * i + 3)
        gp = jnp.dot(grad_buf[part, :], wout[...], preferred_element_type=F32)
        if i == 0:
            win[...] = win_raw[...].T
        else:
            add_up(*pending)
        left = gp.T.astype(BF16)
        if i < chunks - 1:
            wait(2 * i + 1)
            start(2 * i + 4)
            xp = jnp.dot(act_buf[part, :], win[...], preferred_element_type=F32)
        else:
            pieces = []
            for h, load in enumerate(loads[2 * i + 1]):
                load.wait()
                piece = pl.ds(i * rows + h * (rows // 2), rows // 2)
                pieces.append(jnp.dot(act_buf[piece, :], win[...], preferred_element_type=F32))
            xp = jnp.concatenate(pieces, axis=0)
        pending = (i, left, xp)
    add_up(*pending)
    core = lax.rem(grp, 2)
    for x in range(groups // 2):
        send[x] = store[2 * x + 1 - core].astype(BF16)
        keep[x] = store[2 * x + core]


def fold_kernel(keep, came, *rest):
    send, kept = rest[-2:]
    x = lax.axis_index("grp") // 2
    send[...] = (keep[1 - x] + came[1 - x].astype(F32)).astype(BF16)
    kept[...] = keep[x] + came[x].astype(F32)


def combine_kernel(dims, kept, came, *rest):
    half, lines, width = dims
    out, squares, grads = rest[-3:]
    grads[...] = kept[...] + came[...].astype(F32)
    low = lax.broadcasted_iota(jnp.int32, (half, 128), 1) < width
    sums, columns = None, []
    for e in range(0, lines, 2):
        first = grads[pl.ds(e, half, stride=lines), :]
        second = grads[pl.ds(e + 1, half, stride=lines), :]
        line = jnp.concatenate(
            [
                jnp.where(low, first, pltpu.roll(second, width, 1)),
                jnp.where(low, pltpu.roll(first, width, 1), second),
            ],
            axis=0,
        )
        columns.append(line.astype(BF16))
        sums = line * line if sums is None else sums + line * line
    squares[...] = sums
    out[...] = jnp.concatenate(columns, axis=1)


def join_kernel(count, *refs):
    out = refs[-1]
    nq = refs[-2].shape[0]
    for n, ref in enumerate(refs[-1 - count : -1]):
        out[n * nq : (n + 1) * nq, :] = ref[...]


def near_kernel(dims, left, *refs):
    blk = lax.axis_index("blk")
    place = refs[-1]
    for flip, piece in zip(dims, refs[:-1]):
        place[jnp.bitwise_xor(blk, flip)] = lax.dot_general(
            left[...], piece[...], BY_ROWS, preferred_element_type=F32
        )


def scores_kernel(dims, left, squares, near, passed, send, keep, place, result):
    blks, groups = dims
    rows = left[...]
    blk = lax.axis_index("blk")
    nq = near.shape[2]
    place[...] = near[...]
    for n in range(blks // 2 - 2):
        place[jnp.bitwise_xor(blk, 2 * n + 5)] = lax.dot_general(
            rows, passed[n * nq : (n + 1) * nq, :], BY_ROWS, preferred_element_type=F32
        )
    scores = jnp.concatenate([place[b] for b in range(blks)], axis=1)
    width = blks * nq
    owned = scores.shape[0] // groups
    for g in range(groups):
        here = slice(g * owned, (g + 1) * owned)
        result[g, :, :width] = scores[here]
        result[g, :, width:] = squares[here, :]
    x = lax.axis_index("grp") // 2
    for core in range(2):
        send[core] = result[2 * (1 - x) + core]
        keep[core] = result[2 * x + core]


def pass_kernel(keep, came, send, kept):
    core = lax.rem(lax.axis_index("grp"), 2)
    send[...] = keep[1 - core] + came[1 - core]
    kept[...] = keep[core] + came[core]


def finish_kernel(pdim, kept, came, out):
    total = kept[...] + came[...]
    width = out.shape[1]
    mean = jnp.sum(total[:, width:], axis=1, keepdims=True) / pdim
    out[...] = total[:, :width] * lax.rsqrt(mean + EPS)


def small(kernel, out_shape, operands, scratch_shapes=(), name=None):
    one = not isinstance(out_shape, list)
    return pl.pallas_call(
        kernel,
        out_shape=out_shape,
        in_specs=[VMEM] * len(operands),
        out_specs=VMEM if one else [VMEM] * len(out_shape),
        scratch_shapes=list(scratch_shapes),
        compiler_params=pltpu.CompilerParams(vmem_limit_bytes=16 * 2**20),
        name=name,
    )(*operands)


def on_device(blks, groups, acts, out_grads, proj_in, proj_out, lengths, queries):
    _, cands, tokens, depth = acts.shape
    width = proj_in.shape[2]
    far = blks // 2
    pdim = width * width
    lines = width // groups
    nq = queries.shape[0]
    total_q = nq * blks
    owned = cands // groups
    slice_width = pdim // groups
    shape = jax.ShapeDtypeStruct

    def grp_swap(x, k):
        return lax.ppermute(x, "grp", [(g, g ^ k) for g in range(groups)])

    def blk_swap(x, k):
        return lax.ppermute(x, "blk", [(b, b ^ k) for b in range(blks)])

    cut = lax.dynamic_slice(queries, (0, lax.axis_index("grp") * slice_width), (nq, slice_width))
    cut, lens = lax.optimization_barrier((cut, jnp.minimum(lengths, tokens * groups)))
    pieces = [cut, blk_swap(cut, 1), blk_swap(cut, 2), blk_swap(cut, 3)]
    distant = [blk_swap(cut, 2 * k) for k in range(2, far)]

    rows = cands * tokens
    piece = (cands // 2 * lines, 128)
    send, keep = pl.pallas_call(
        functools.partial(grads_kernel, (cands, tokens, width, groups)),
        out_shape=[shape((groups // 2,) + piece, BF16), shape((groups // 2,) + piece, F32)],
        in_specs=[ANY] * 5,
        out_specs=[VMEM] * 2,
        scratch_shapes=[
            pltpu.VMEM((rows, depth), BF16),
            pltpu.VMEM((rows, depth), BF16),
            pltpu.VMEM((width, depth), BF16),
            pltpu.VMEM((width, depth), BF16),
            pltpu.VMEM((depth, width), BF16),
            pltpu.VMEM((depth, width), BF16),
            pltpu.SMEM((cands,), jnp.int32),
            pltpu.VMEM((groups,) + piece, F32),
            pltpu.SemaphoreType.DMA((2, cands // 2)),
            pltpu.SemaphoreType.DMA((3,)),
        ],
        compiler_params=pltpu.CompilerParams(vmem_limit_bytes=GRANT * 2**10),
        cost_estimate=pl.CostEstimate(
            flops=16 * rows * depth * width, bytes_accessed=4 * rows * depth, transcendentals=0
        ),
        name="grads",
    )(
        lens,
        acts.reshape(rows, depth),
        out_grads.reshape(rows, depth),
        proj_in[0].T,
        proj_out[0].T,
    )
    joined = small(
        functools.partial(join_kernel, far - 2),
        shape(((far - 2) * nq, slice_width), BF16),
        (*pieces[1:], keep, *distant),
        name="join",
    )
    send, kept = small(
        fold_kernel,
        [shape(piece, BF16), shape(piece, F32)],
        (keep, grp_swap(send, 1), joined),
        name="fold",
    )
    passed = blk_swap(joined, 1)
    own, squares = small(
        functools.partial(combine_kernel, (cands // 2, lines, width)),
        [shape((cands, slice_width), BF16), shape((cands, 128), F32)],
        (kept, grp_swap(send, 2)),
        [pltpu.VMEM(piece, F32)],
        name="combine",
    )
    near = small(
        functools.partial(near_kernel, [0, 1, 2, 3] + [2 * k for k in range(2, far)]),
        shape((blks, cands, nq), F32),
        (own, *pieces, *distant),
        name="near",
    )
    line = (owned, total_q + 128)
    send, keep = small(
        functools.partial(scores_kernel, (blks, groups)),
        [shape((groups // 2,) + line, F32)] * 2,
        (own, squares, near, passed),
        [pltpu.VMEM((blks, cands, nq), F32), pltpu.VMEM((groups,) + line, F32)],
        name="scores",
    )
    send, kept = small(pass_kernel, [shape(line, F32)] * 2, (keep, grp_swap(send, 2)), name="pass")
    return small(
        functools.partial(finish_kernel, pdim),
        shape((owned, total_q), F32),
        (kept, grp_swap(send, 1)),
        name="finish",
    )


def solution(mesh):
    in_specs = (
        P(None, "blk", "grp", None),
        P(None, "blk", "grp", None),
        P(),
        P(),
        P("blk"),
        P("blk", None),
    )
    return jax.shard_map(
        functools.partial(on_device, mesh.shape["blk"], mesh.shape["grp"]),
        mesh=mesh,
        in_specs=in_specs,
        out_specs=P(("blk", "grp"), None),
        check_vma=False,
    )
```

```python
import functools

import jax
import jax.numpy as jnp
from jax import lax
from jax.experimental import pallas as pl
from jax.experimental.pallas import tpu as pltpu
from jax.sharding import PartitionSpec as P

EPS = 1e-06
GRANT = 54784
F32 = jnp.float32
BF16 = jnp.bfloat16
VMEM = pl.BlockSpec(memory_space=pltpu.VMEM)
ANY = pl.BlockSpec(memory_space=pl.ANY)
BY_ROWS = (((1,), (1,)), ((), ()))


def grads_kernel(dims, lens_in, acts, grads, w_in, w_out, send, keep, *scratch):
    cands, tokens, width, groups = dims
    act_buf, grad_buf, win_raw, wout_raw, win, wout, lens, store, sems, wsems = scratch
    chunks = cands // 4
    rows = 4 * tokens
    loads = []
    for i in range(chunks):
        for side, (source, buf) in enumerate(((grads, grad_buf), (acts, act_buf))):
            cuts = 2 if side == 1 and i == chunks - 1 else 1
            loads.append(
                [
                    pltpu.make_async_copy(source.at[part], buf.at[part], sems.at[side, i + h])
                    for h in range(cuts)
                    for part in [pl.ds(i * rows + h * (rows // 2), rows // cuts)]
                ]
            )

    def start(n):
        if n < len(loads):
            for load in loads[n]:
                load.start()

    def wait(n):
        for load in loads[n]:
            load.wait()

    load_lens = pltpu.make_async_copy(lens_in, lens, wsems.at[2])
    load_wout = pltpu.make_async_copy(w_out, wout_raw, wsems.at[0])
    load_win = pltpu.make_async_copy(w_in, win_raw, wsems.at[1])
    load_wout.start()
    load_win.start()
    load_lens.start()
    for n in range(2):
        start(n)
    grp = lax.axis_index("grp")
    lines = width // groups
    position = lax.broadcasted_iota(jnp.int32, (tokens, width), 0) + grp * tokens
    row_blk = lax.broadcasted_iota(jnp.int32, (rows, rows), 0) // tokens
    col_blk = lax.broadcasted_iota(jnp.int32, (rows, 4 * width), 1) // width
    diagonal = row_blk == col_blk // 2 + 2 * (col_blk % 2)

    def add_up(i, left, xp):
        used = []
        for j in range(4):
            used.append(jnp.where(position < lens[4 * i + j], xp[j * tokens : (j + 1) * tokens], 0.0))
        wide = jnp.concatenate([jnp.concatenate(used, axis=0)] * 4, axis=1)
        right = jnp.where(diagonal, wide, 0.0).astype(BF16)
        sums = jnp.dot(left, right, preferred_element_type=F32)
        for t in range(2):
            there = slice((2 * i + t) * lines, (2 * i + t + 1) * lines)
            for s in range(groups):
                store[s, there, :] = sums[s * lines : (s + 1) * lines, t * 128 : (t + 1) * 128]

    load_wout.wait()
    wout[...] = wout_raw[...].T
    load_win.wait()
    load_lens.wait()
    pending = None
    for i in range(chunks):
        part = pl.ds(i * rows, rows)
        wait(2 * i)
        start(2 * i + 2)
        gp = jnp.dot(grad_buf[part, :], wout[...], preferred_element_type=F32)
        if i == 0:
            win[...] = win_raw[...].T
        else:
            add_up(*pending)
        left = gp.T.astype(BF16)
        if i < chunks - 1:
            wait(2 * i + 1)
            start(2 * i + 3)
            xp = jnp.dot(act_buf[part, :], win[...], preferred_element_type=F32)
        else:
            pieces = []
            for h, load in enumerate(loads[2 * i + 1]):
                load.wait()
                piece = pl.ds(i * rows + h * (rows // 2), rows // 2)
                pieces.append(jnp.dot(act_buf[piece, :], win[...], preferred_element_type=F32))
            xp = jnp.concatenate(pieces, axis=0)
        pending = (i, left, xp)
    add_up(*pending)
    core = lax.rem(grp, 2)
    for x in range(groups // 2):
        send[x] = store[2 * x + 1 - core].astype(BF16)
        keep[x] = store[2 * x + core]


def fold_kernel(keep, came, *rest):
    send, kept = rest[-2:]
    x = lax.axis_index("grp") // 2
    send[...] = (keep[1 - x] + came[1 - x].astype(F32)).astype(BF16)
    kept[...] = keep[x] + came[x].astype(F32)


def combine_kernel(dims, kept, came, *rest):
    half, lines, width = dims
    out, squares, grads = rest[-3:]
    grads[...] = kept[...] + came[...].astype(F32)
    low = lax.broadcasted_iota(jnp.int32, (half, 128), 1) < width
    sums, columns = None, []
    for e in range(0, lines, 2):
        first = grads[pl.ds(e, half, stride=lines), :]
        second = grads[pl.ds(e + 1, half, stride=lines), :]
        line = jnp.concatenate(
            [
                jnp.where(low, first, pltpu.roll(second, width, 1)),
                jnp.where(low, pltpu.roll(first, width, 1), second),
            ],
            axis=0,
        )
        columns.append(line.astype(BF16))
        sums = line * line if sums is None else sums + line * line
    squares[...] = sums
    out[...] = jnp.concatenate(columns, axis=1)


def join_kernel(count, *refs):
    out = refs[-1]
    nq = refs[-2].shape[0]
    for n, ref in enumerate(refs[-1 - count : -1]):
        out[n * nq : (n + 1) * nq, :] = ref[...]


def near_kernel(dims, left, *refs):
    blk = lax.axis_index("blk")
    place = refs[-1]
    for flip, piece in zip(dims, refs[:-1]):
        place[jnp.bitwise_xor(blk, flip)] = lax.dot_general(
            left[...], piece[...], BY_ROWS, preferred_element_type=F32
        )


def scores_kernel(dims, left, squares, near, late, passed, send, keep, place, result):
    blks, groups = dims
    rows = left[...]
    blk = lax.axis_index("blk")
    nq = near.shape[2]
    place[...] = near[...]
    place[jnp.bitwise_xor(blk, 2)] = lax.dot_general(
        rows, late[...], BY_ROWS, preferred_element_type=F32
    )
    for n in range(blks // 2 - 2):
        place[jnp.bitwise_xor(blk, 2 * n + 5)] = lax.dot_general(
            rows, passed[n * nq : (n + 1) * nq, :], BY_ROWS, preferred_element_type=F32
        )
    scores = jnp.concatenate([place[b] for b in range(blks)], axis=1)
    width = blks * nq
    half = scores.shape[0] // 2
    owned = half // groups
    for g in range(groups):
        for h in range(2):
            here = slice(h * half + g * owned, h * half + (g + 1) * owned)
            there = slice(h * owned, (h + 1) * owned)
            result[g, there, :width] = scores[here]
            result[g, there, width:] = squares[here, :]
    x = lax.axis_index("grp") // 2
    for core in range(2):
        send[core] = result[2 * (1 - x) + core]
        keep[core] = result[2 * x + core]


def pass_kernel(keep, came, send, kept):
    core = lax.rem(lax.axis_index("grp"), 2)
    send[...] = keep[1 - core] + came[1 - core]
    kept[...] = keep[core] + came[core]


def finish_kernel(pdim, kept, came, out):
    total = kept[...] + came[...]
    width = out.shape[1]
    mean = jnp.sum(total[:, width:], axis=1, keepdims=True) / pdim
    out[...] = total[:, :width] * lax.rsqrt(mean + EPS)


def small(kernel, out_shape, operands, scratch_shapes=(), name=None):
    one = not isinstance(out_shape, list)
    return pl.pallas_call(
        kernel,
        out_shape=out_shape,
        in_specs=[VMEM] * len(operands),
        out_specs=VMEM if one else [VMEM] * len(out_shape),
        scratch_shapes=list(scratch_shapes),
        compiler_params=pltpu.CompilerParams(vmem_limit_bytes=16 * 2**20),
        name=name,
    )(*operands)


def on_device(blks, groups, acts, out_grads, proj_in, proj_out, lengths, queries):
    _, cands, tokens, depth = acts.shape
    width = proj_in.shape[2]
    far = blks // 2
    pdim = width * width
    lines = width // groups
    nq = queries.shape[0]
    total_q = nq * blks
    owned = cands // groups
    slice_width = pdim // groups
    shape = jax.ShapeDtypeStruct

    def grp_swap(x, k):
        return lax.ppermute(x, "grp", [(g, g ^ k) for g in range(groups)])

    def blk_swap(x, k):
        return lax.ppermute(x, "blk", [(b, b ^ k) for b in range(blks)])

    cut = lax.dynamic_slice(queries, (0, lax.axis_index("grp") * slice_width), (nq, slice_width))
    cut, lens = lax.optimization_barrier((cut, jnp.minimum(lengths, tokens * groups)))
    pieces = [cut, blk_swap(cut, 1), blk_swap(cut, 3)]
    distant = [blk_swap(cut, 2 * k) for k in range(2, far)]

    rows = cands * tokens
    piece = (cands // 2 * lines, 128)
    send, keep = pl.pallas_call(
        functools.partial(grads_kernel, (cands, tokens, width, groups)),
        out_shape=[shape((groups // 2,) + piece, BF16), shape((groups // 2,) + piece, F32)],
        in_specs=[ANY] * 5,
        out_specs=[VMEM] * 2,
        scratch_shapes=[
            pltpu.VMEM((rows, depth), BF16),
            pltpu.VMEM((rows, depth), BF16),
            pltpu.VMEM((width, depth), BF16),
            pltpu.VMEM((width, depth), BF16),
            pltpu.VMEM((depth, width), BF16),
            pltpu.VMEM((depth, width), BF16),
            pltpu.SMEM((cands,), jnp.int32),
            pltpu.VMEM((groups,) + piece, F32),
            pltpu.SemaphoreType.DMA((2, cands // 4 + 1)),
            pltpu.SemaphoreType.DMA((3,)),
        ],
        compiler_params=pltpu.CompilerParams(vmem_limit_bytes=GRANT * 2**10),
        cost_estimate=pl.CostEstimate(
            flops=16 * rows * depth * width, bytes_accessed=4 * rows * depth, transcendentals=0
        ),
        name="grads",
    )(
        lens,
        acts.reshape(rows, depth),
        out_grads.reshape(rows, depth),
        proj_in[0].T,
        proj_out[0].T,
    )
    joined = small(
        functools.partial(join_kernel, far - 2),
        shape(((far - 2) * nq, slice_width), BF16),
        (*pieces[1:], keep, *distant),
        name="join",
    )
    late, joined = lax.optimization_barrier((cut, joined))
    late = blk_swap(late, 2)
    send, kept = small(
        fold_kernel,
        [shape(piece, BF16), shape(piece, F32)],
        (keep, grp_swap(send, 1), joined),
        name="fold",
    )
    passed = blk_swap(joined, 1)
    own, squares = small(
        functools.partial(combine_kernel, (cands // 2, lines, width)),
        [shape((cands, slice_width), BF16), shape((cands, 128), F32)],
        (kept, grp_swap(send, 2)),
        [pltpu.VMEM(piece, F32)],
        name="combine",
    )
    near = small(
        functools.partial(near_kernel, [0, 1, 3] + [2 * k for k in range(2, far)]),
        shape((blks, cands, nq), F32),
        (own, *pieces, *distant),
        name="near",
    )
    line = (owned, total_q + 128)
    send, keep = small(
        functools.partial(scores_kernel, (blks, groups)),
        [shape((groups // 2,) + line, F32)] * 2,
        (own, squares, near, late, passed),
        [pltpu.VMEM((blks, cands, nq), F32), pltpu.VMEM((groups,) + line, F32)],
        name="scores",
    )
    send, kept = small(pass_kernel, [shape(line, F32)] * 2, (keep, grp_swap(send, 2)), name="pass")
    return small(
        functools.partial(finish_kernel, pdim),
        shape((owned, total_q), F32),
        (kept, grp_swap(send, 1)),
        name="finish",
    )


def solution(mesh):
    in_specs = (
        P(None, "blk", "grp", None),
        P(None, "blk", "grp", None),
        P(),
        P(),
        P("blk"),
        P("blk", None),
    )
    return jax.shard_map(
        functools.partial(on_device, mesh.shape["blk"], mesh.shape["grp"]),
        mesh=mesh,
        in_specs=in_specs,
        out_specs=P(("blk", "grp"), None),
        check_vma=False,
    )
```

```python
import functools

import jax
import jax.numpy as jnp
from jax import lax
from jax.experimental import pallas as pl
from jax.experimental.pallas import tpu as pltpu
from jax.sharding import PartitionSpec as P

EPS = 1e-06
GRANT = 54784
F32 = jnp.float32
BF16 = jnp.bfloat16
VMEM = pl.BlockSpec(memory_space=pltpu.VMEM)
ANY = pl.BlockSpec(memory_space=pl.ANY)
BY_ROWS = (((1,), (1,)), ((), ()))


def grads_kernel(dims, lens_in, acts, grads, w_in, w_out, send, keep, *scratch):
    cands, tokens, width, groups = dims
    act_buf, grad_buf, win_raw, wout_raw, win, wout, lens, store, sems, wsems = scratch
    chunks = cands // 4
    rows = 4 * tokens
    loads = []
    for i in range(chunks):
        for side, (source, buf) in enumerate(((grads, grad_buf), (acts, act_buf))):
            parts = [pl.ds((2 * i + h) * (rows // 2), rows // 2) for h in range(2)]
            loads.append(
                [
                    pltpu.make_async_copy(source.at[part], buf.at[part], sems.at[side, 2 * i + h])
                    for h, part in enumerate(parts)
                ]
            )

    def start(n):
        if n < len(loads):
            for load in loads[n]:
                load.start()

    def wait(n):
        for load in loads[n]:
            load.wait()

    load_lens = pltpu.make_async_copy(lens_in, lens, wsems.at[2])
    load_wout = pltpu.make_async_copy(w_out, wout_raw, wsems.at[0])
    load_win = pltpu.make_async_copy(w_in, win_raw, wsems.at[1])
    load_wout.start()
    load_win.start()
    load_lens.start()
    for n in range(3):
        start(n)
    grp = lax.axis_index("grp")
    lines = width // groups
    position = lax.broadcasted_iota(jnp.int32, (tokens, width), 0) + grp * tokens
    row_blk = lax.broadcasted_iota(jnp.int32, (rows, rows), 0) // tokens
    col_blk = lax.broadcasted_iota(jnp.int32, (rows, 4 * width), 1) // width
    diagonal = row_blk == col_blk // 2 + 2 * (col_blk % 2)

    def add_up(i, left, xp):
        used = []
        for j in range(4):
            used.append(jnp.where(position < lens[4 * i + j], xp[j * tokens : (j + 1) * tokens], 0.0))
        wide = jnp.concatenate([jnp.concatenate(used, axis=0)] * 4, axis=1)
        right = jnp.where(diagonal, wide, 0.0).astype(BF16)
        sums = jnp.dot(left, right, preferred_element_type=F32)
        for t in range(2):
            there = slice((2 * i + t) * lines, (2 * i + t + 1) * lines)
            for s in range(groups):
                store[s, there, :] = sums[s * lines : (s + 1) * lines, t * 128 : (t + 1) * 128]

    load_wout.wait()
    wout[...] = wout_raw[...].T
    load_win.wait()
    load_lens.wait()
    pending = None
    for i in range(chunks):
        part = pl.ds(i * rows, rows)
        wait(2 * i)
        start(2 * i + 3)
        gp = jnp.dot(grad_buf[part, :], wout[...], preferred_element_type=F32)
        if i == 0:
            win[...] = win_raw[...].T
        else:
            add_up(*pending)
        left = gp.T.astype(BF16)
        if i < chunks - 1:
            wait(2 * i + 1)
            start(2 * i + 4)
            xp = jnp.dot(act_buf[part, :], win[...], preferred_element_type=F32)
        else:
            pieces = []
            for h, load in enumerate(loads[2 * i + 1]):
                load.wait()
                piece = pl.ds(i * rows + h * (rows // 2), rows // 2)
                pieces.append(jnp.dot(act_buf[piece, :], win[...], preferred_element_type=F32))
            xp = jnp.concatenate(pieces, axis=0)
        pending = (i, left, xp)
    add_up(*pending)
    core = lax.rem(grp, 2)
    for x in range(groups // 2):
        send[x] = store[2 * x + 1 - core]
        keep[x] = store[2 * x + core]


def fold_kernel(keep, came, *rest):
    send, kept = rest[-2:]
    x = lax.axis_index("grp") // 2
    send[...] = (keep[1 - x] + came[1 - x]).astype(BF16)
    kept[...] = keep[x] + came[x]


def combine_kernel(dims, kept, came, *rest):
    half, lines, width = dims
    out, squares, grads = rest[-3:]
    grads[...] = kept[...] + came[...].astype(F32)
    low = lax.broadcasted_iota(jnp.int32, (half, 128), 1) < width
    sums, columns = None, []
    for e in range(0, lines, 2):
        first = grads[pl.ds(e, half, stride=lines), :]
        second = grads[pl.ds(e + 1, half, stride=lines), :]
        line = jnp.concatenate(
            [
                jnp.where(low, first, pltpu.roll(second, width, 1)),
                jnp.where(low, pltpu.roll(first, width, 1), second),
            ],
            axis=0,
        )
        columns.append(line.astype(BF16))
        sums = line * line if sums is None else sums + line * line
    squares[...] = sums
    out[...] = jnp.concatenate(columns, axis=1)


def join_kernel(count, *refs):
    out = refs[-1]
    nq = refs[-2].shape[0]
    for n, ref in enumerate(refs[-1 - count : -1]):
        out[n * nq : (n + 1) * nq, :] = ref[...]


def near_kernel(dims, left, *refs):
    blk = lax.axis_index("blk")
    place = refs[-1]
    for flip, piece in zip(dims, refs[:-1]):
        place[jnp.bitwise_xor(blk, flip)] = lax.dot_general(
            left[...], piece[...], BY_ROWS, preferred_element_type=F32
        )


def scores_kernel(dims, left, squares, near, late, passed, send, keep, place, result):
    blks, groups = dims
    rows = left[...]
    blk = lax.axis_index("blk")
    nq = near.shape[2]
    place[...] = near[...]
    place[jnp.bitwise_xor(blk, 2)] = lax.dot_general(
        rows, late[...], BY_ROWS, preferred_element_type=F32
    )
    for n in range(blks // 2 - 2):
        place[jnp.bitwise_xor(blk, 2 * n + 5)] = lax.dot_general(
            rows, passed[n * nq : (n + 1) * nq, :], BY_ROWS, preferred_element_type=F32
        )
    scores = jnp.concatenate([place[b] for b in range(blks)], axis=1)
    width = blks * nq
    half = scores.shape[0] // 2
    owned = half // groups
    for g in range(groups):
        for h in range(2):
            here = slice(h * half + g * owned, h * half + (g + 1) * owned)
            there = slice(h * owned, (h + 1) * owned)
            result[g, there, :width] = scores[here]
            result[g, there, width:] = squares[here, :]
    x = lax.axis_index("grp") // 2
    for core in range(2):
        send[core] = result[2 * (1 - x) + core]
        keep[core] = result[2 * x + core]


def pass_kernel(keep, came, send, kept):
    core = lax.rem(lax.axis_index("grp"), 2)
    send[...] = keep[1 - core] + came[1 - core]
    kept[...] = keep[core] + came[core]


def finish_kernel(pdim, kept, came, out):
    total = kept[...] + came[...]
    width = out.shape[1]
    mean = jnp.sum(total[:, width:], axis=1, keepdims=True) / pdim
    out[...] = total[:, :width] * lax.rsqrt(mean + EPS)


def small(kernel, out_shape, operands, scratch_shapes=(), name=None):
    one = not isinstance(out_shape, list)
    return pl.pallas_call(
        kernel,
        out_shape=out_shape,
        in_specs=[VMEM] * len(operands),
        out_specs=VMEM if one else [VMEM] * len(out_shape),
        scratch_shapes=list(scratch_shapes),
        compiler_params=pltpu.CompilerParams(vmem_limit_bytes=16 * 2**20),
        name=name,
    )(*operands)


def on_device(blks, groups, acts, out_grads, proj_in, proj_out, lengths, queries):
    _, cands, tokens, depth = acts.shape
    width = proj_in.shape[2]
    far = blks // 2
    pdim = width * width
    lines = width // groups
    nq = queries.shape[0]
    total_q = nq * blks
    owned = cands // groups
    slice_width = pdim // groups
    shape = jax.ShapeDtypeStruct

    def grp_swap(x, k):
        return lax.ppermute(x, "grp", [(g, g ^ k) for g in range(groups)])

    def blk_swap(x, k):
        return lax.ppermute(x, "blk", [(b, b ^ k) for b in range(blks)])

    cut = lax.dynamic_slice(queries, (0, lax.axis_index("grp") * slice_width), (nq, slice_width))
    cut, lens = lax.optimization_barrier((cut, jnp.minimum(lengths, tokens * groups)))
    pieces = [cut, blk_swap(cut, 1), blk_swap(cut, 3)]
    distant = [blk_swap(cut, 2 * k) for k in range(2, far)]

    rows = cands * tokens
    piece = (cands // 2 * lines, 128)
    send, keep = pl.pallas_call(
        functools.partial(grads_kernel, (cands, tokens, width, groups)),
        out_shape=[shape((groups // 2,) + piece, F32)] * 2,
        in_specs=[ANY] * 5,
        out_specs=[VMEM] * 2,
        scratch_shapes=[
            pltpu.VMEM((rows, depth), BF16),
            pltpu.VMEM((rows, depth), BF16),
            pltpu.VMEM((width, depth), BF16),
            pltpu.VMEM((width, depth), BF16),
            pltpu.VMEM((depth, width), BF16),
            pltpu.VMEM((depth, width), BF16),
            pltpu.SMEM((cands,), jnp.int32),
            pltpu.VMEM((groups,) + piece, F32),
            pltpu.SemaphoreType.DMA((2, cands // 2)),
            pltpu.SemaphoreType.DMA((3,)),
        ],
        compiler_params=pltpu.CompilerParams(vmem_limit_bytes=GRANT * 2**10),
        cost_estimate=pl.CostEstimate(
            flops=16 * rows * depth * width, bytes_accessed=4 * rows * depth, transcendentals=0
        ),
        name="grads",
    )(
        lens,
        acts.reshape(rows, depth),
        out_grads.reshape(rows, depth),
        proj_in[0].T,
        proj_out[0].T,
    )
    joined = small(
        functools.partial(join_kernel, far - 2),
        shape(((far - 2) * nq, slice_width), BF16),
        (*pieces[1:], keep, *distant),
        name="join",
    )
    late, joined = lax.optimization_barrier((cut, joined))
    late = blk_swap(late, 2)
    send, kept = small(
        fold_kernel,
        [shape(piece, BF16), shape(piece, F32)],
        (keep, grp_swap(send, 1), joined),
        name="fold",
    )
    passed = blk_swap(joined, 1)
    own, squares = small(
        functools.partial(combine_kernel, (cands // 2, lines, width)),
        [shape((cands, slice_width), BF16), shape((cands, 128), F32)],
        (kept, grp_swap(send, 2)),
        [pltpu.VMEM(piece, F32)],
        name="combine",
    )
    near = small(
        functools.partial(near_kernel, [0, 1, 3] + [2 * k for k in range(2, far)]),
        shape((blks, cands, nq), F32),
        (own, *pieces, *distant),
        name="near",
    )
    line = (owned, total_q + 128)
    send, keep = small(
        functools.partial(scores_kernel, (blks, groups)),
        [shape((groups // 2,) + line, F32)] * 2,
        (own, squares, near, late, passed),
        [pltpu.VMEM((blks, cands, nq), F32), pltpu.VMEM((groups,) + line, F32)],
        name="scores",
    )
    send, kept = small(pass_kernel, [shape(line, F32)] * 2, (keep, grp_swap(send, 2)), name="pass")
    return small(
        functools.partial(finish_kernel, pdim),
        shape((owned, total_q), F32),
        (kept, grp_swap(send, 1)),
        name="finish",
    )


def solution(mesh):
    in_specs = (
        P(None, "blk", "grp", None),
        P(None, "blk", "grp", None),
        P(),
        P(),
        P("blk"),
        P("blk", None),
    )
    return jax.shard_map(
        functools.partial(on_device, mesh.shape["blk"], mesh.shape["grp"]),
        mesh=mesh,
        in_specs=in_specs,
        out_specs=P(("blk", "grp"), None),
        check_vma=False,
    )
```

```python
import functools

import jax
import jax.numpy as jnp
from jax import lax
from jax.experimental import pallas as pl
from jax.experimental.pallas import tpu as pltpu
from jax.sharding import PartitionSpec as P

EPS = 1e-06
GRANT = 54784
F32 = jnp.float32
BF16 = jnp.bfloat16
VMEM = pl.BlockSpec(memory_space=pltpu.VMEM)
ANY = pl.BlockSpec(memory_space=pl.ANY)
BY_ROWS = (((1,), (1,)), ((), ()))


def grads_kernel(dims, lens_in, acts, grads, w_in, w_out, send, keep, *scratch):
    cands, tokens, width, groups = dims
    act_buf, grad_buf, win_raw, wout_raw, win, wout, lens, store, sems, wsems = scratch
    chunks = cands // 4
    rows = 4 * tokens
    loads = []
    for i in range(chunks):
        for side, (source, buf) in enumerate(((grads, grad_buf), (acts, act_buf))):
            parts = [pl.ds((2 * i + h) * (rows // 2), rows // 2) for h in range(2)]
            loads.append(
                [
                    pltpu.make_async_copy(source.at[part], buf.at[part], sems.at[side, 2 * i + h])
                    for h, part in enumerate(parts)
                ]
            )

    def start(n):
        if n < len(loads):
            for load in loads[n]:
                load.start()

    def wait(n):
        for load in loads[n]:
            load.wait()

    load_lens = pltpu.make_async_copy(lens_in, lens, wsems.at[2])
    load_wout = pltpu.make_async_copy(w_out, wout_raw, wsems.at[0])
    load_win = pltpu.make_async_copy(w_in, win_raw, wsems.at[1])
    load_wout.start()
    load_win.start()
    load_lens.start()
    for n in range(3):
        start(n)
    grp = lax.axis_index("grp")
    lines = width // groups
    position = lax.broadcasted_iota(jnp.int32, (tokens, width), 0) + grp * tokens
    row_blk = lax.broadcasted_iota(jnp.int32, (rows, rows), 0) // tokens
    col_blk = lax.broadcasted_iota(jnp.int32, (rows, 4 * width), 1) // width
    diagonal = row_blk == col_blk // 2 + 2 * (col_blk % 2)

    def add_up(i, left, xp):
        used = []
        for j in range(4):
            used.append(jnp.where(position < lens[4 * i + j], xp[j * tokens : (j + 1) * tokens], 0.0))
        wide = jnp.concatenate([jnp.concatenate(used, axis=0)] * 4, axis=1)
        right = jnp.where(diagonal, wide, 0.0).astype(BF16)
        sums = jnp.dot(left, right, preferred_element_type=F32)
        for t in range(2):
            there = slice((2 * i + t) * lines, (2 * i + t + 1) * lines)
            for s in range(groups):
                store[s, there, :] = sums[s * lines : (s + 1) * lines, t * 128 : (t + 1) * 128]

    load_wout.wait()
    wout[...] = wout_raw[...].T
    load_win.wait()
    load_lens.wait()
    pending = None
    for i in range(chunks):
        part = pl.ds(i * rows, rows)
        wait(2 * i)
        start(2 * i + 3)
        gp = jnp.dot(grad_buf[part, :], wout[...], preferred_element_type=F32)
        if i == 0:
            win[...] = win_raw[...].T
        else:
            add_up(*pending)
        left = gp.T.astype(BF16)
        if i < chunks - 1:
            wait(2 * i + 1)
            start(2 * i + 4)
            xp = jnp.dot(act_buf[part, :], win[...], preferred_element_type=F32)
        else:
            pieces = []
            for h, load in enumerate(loads[2 * i + 1]):
                load.wait()
                piece = pl.ds(i * rows + h * (rows // 2), rows // 2)
                pieces.append(jnp.dot(act_buf[piece, :], win[...], preferred_element_type=F32))
            xp = jnp.concatenate(pieces, axis=0)
        pending = (i, left, xp)
    add_up(*pending)
    core = lax.rem(grp, 2)
    for x in range(groups // 2):
        send[x] = store[2 * x + 1 - core]
        keep[x] = store[2 * x + core]


def fold_kernel(keep, came, *rest):
    send, kept = rest[-2:]
    x = lax.axis_index("grp") // 2
    send[...] = (keep[1 - x] + came[1 - x]).astype(BF16)
    kept[...] = keep[x] + came[x]


def combine_kernel(dims, kept, came, *rest):
    half, lines, width = dims
    out, squares, grads = rest[-3:]
    grads[...] = kept[...] + came[...].astype(F32)
    low = lax.broadcasted_iota(jnp.int32, (half, 128), 1) < width
    sums, columns = None, []
    for e in range(0, lines, 2):
        first = grads[pl.ds(e, half, stride=lines), :]
        second = grads[pl.ds(e + 1, half, stride=lines), :]
        line = jnp.concatenate(
            [
                jnp.where(low, first, pltpu.roll(second, width, 1)),
                jnp.where(low, pltpu.roll(first, width, 1), second),
            ],
            axis=0,
        )
        columns.append(line.astype(BF16))
        sums = line * line if sums is None else sums + line * line
    squares[...] = sums
    out[...] = jnp.concatenate(columns, axis=1)


def join_kernel(count, *refs):
    out = refs[-1]
    nq = refs[-2].shape[0]
    for n, ref in enumerate(refs[-1 - count : -1]):
        out[n * nq : (n + 1) * nq, :] = ref[...]


def near_kernel(dims, left, *refs):
    blk = lax.axis_index("blk")
    place = refs[-1]
    for flip, piece in zip(dims, refs[:-1]):
        place[jnp.bitwise_xor(blk, flip)] = lax.dot_general(
            left[...], piece[...], BY_ROWS, preferred_element_type=F32
        )


def scores_kernel(dims, left, squares, near, late, passed, *rest):
    blks, groups = dims
    outs = rest[:groups]
    place, result = rest[groups:]
    rows = left[...]
    blk = lax.axis_index("blk")
    nq = near.shape[2]
    place[...] = near[...]
    place[jnp.bitwise_xor(blk, 2)] = lax.dot_general(
        rows, late[...], BY_ROWS, preferred_element_type=F32
    )
    for n in range(blks // 2 - 2):
        place[jnp.bitwise_xor(blk, 2 * n + 5)] = lax.dot_general(
            rows, passed[n * nq : (n + 1) * nq, :], BY_ROWS, preferred_element_type=F32
        )
    scores = jnp.concatenate([place[b] for b in range(blks)], axis=1)
    width = blks * nq
    half = scores.shape[0] // 2
    owned = half // groups
    for g in range(groups):
        for h in range(2):
            here = slice(h * half + g * owned, h * half + (g + 1) * owned)
            there = slice(h * owned, (h + 1) * owned)
            result[g, there, :width] = scores[here]
            result[g, there, width:] = squares[here, :]
    grp = lax.axis_index("grp")
    for k in range(groups):
        outs[k][...] = result[jnp.bitwise_xor(grp, k)]


def finish_kernel(pdim, *refs):
    out = refs[-1]
    total = refs[0][...]
    for ref in refs[1:-1]:
        total = total + ref[...]
    width = out.shape[1]
    mean = jnp.sum(total[:, width:], axis=1, keepdims=True) / pdim
    out[...] = total[:, :width] * lax.rsqrt(mean + EPS)


def small(kernel, out_shape, operands, scratch_shapes=(), name=None):
    one = not isinstance(out_shape, list)
    return pl.pallas_call(
        kernel,
        out_shape=out_shape,
        in_specs=[VMEM] * len(operands),
        out_specs=VMEM if one else [VMEM] * len(out_shape),
        scratch_shapes=list(scratch_shapes),
        compiler_params=pltpu.CompilerParams(vmem_limit_bytes=16 * 2**20),
        name=name,
    )(*operands)


def on_device(blks, groups, acts, out_grads, proj_in, proj_out, lengths, queries):
    _, cands, tokens, depth = acts.shape
    width = proj_in.shape[2]
    far = blks // 2
    pdim = width * width
    lines = width // groups
    nq = queries.shape[0]
    total_q = nq * blks
    owned = cands // groups
    slice_width = pdim // groups
    shape = jax.ShapeDtypeStruct

    def grp_swap(x, k):
        return lax.ppermute(x, "grp", [(g, g ^ k) for g in range(groups)])

    def blk_swap(x, k):
        return lax.ppermute(x, "blk", [(b, b ^ k) for b in range(blks)])

    cut = lax.dynamic_slice(queries, (0, lax.axis_index("grp") * slice_width), (nq, slice_width))
    cut, lens = lax.optimization_barrier((cut, jnp.minimum(lengths, tokens * groups)))
    pieces = [cut, blk_swap(cut, 1), blk_swap(cut, 3)]
    distant = [blk_swap(cut, 2 * k) for k in range(2, far)]

    rows = cands * tokens
    piece = (cands // 2 * lines, 128)
    send, keep = pl.pallas_call(
        functools.partial(grads_kernel, (cands, tokens, width, groups)),
        out_shape=[shape((groups // 2,) + piece, F32)] * 2,
        in_specs=[ANY] * 5,
        out_specs=[VMEM] * 2,
        scratch_shapes=[
            pltpu.VMEM((rows, depth), BF16),
            pltpu.VMEM((rows, depth), BF16),
            pltpu.VMEM((width, depth), BF16),
            pltpu.VMEM((width, depth), BF16),
            pltpu.VMEM((depth, width), BF16),
            pltpu.VMEM((depth, width), BF16),
            pltpu.SMEM((cands,), jnp.int32),
            pltpu.VMEM((groups,) + piece, F32),
            pltpu.SemaphoreType.DMA((2, cands // 2)),
            pltpu.SemaphoreType.DMA((3,)),
        ],
        compiler_params=pltpu.CompilerParams(vmem_limit_bytes=GRANT * 2**10),
        cost_estimate=pl.CostEstimate(
            flops=16 * rows * depth * width, bytes_accessed=4 * rows * depth, transcendentals=0
        ),
        name="grads",
    )(
        lens,
        acts.reshape(rows, depth),
        out_grads.reshape(rows, depth),
        proj_in[0].T,
        proj_out[0].T,
    )
    joined = small(
        functools.partial(join_kernel, far - 2),
        shape(((far - 2) * nq, slice_width), BF16),
        (*pieces[1:], keep, *distant),
        name="join",
    )
    late, joined = lax.optimization_barrier((cut, joined))
    late = blk_swap(late, 2)
    send, kept = small(
        fold_kernel,
        [shape(piece, BF16), shape(piece, F32)],
        (keep, grp_swap(send, 1), joined),
        name="fold",
    )
    passed = blk_swap(joined, 1)
    own, squares = small(
        functools.partial(combine_kernel, (cands // 2, lines, width)),
        [shape((cands, slice_width), BF16), shape((cands, 128), F32)],
        (kept, grp_swap(send, 2)),
        [pltpu.VMEM(piece, F32)],
        name="combine",
    )
    near = small(
        functools.partial(near_kernel, [0, 1, 3] + [2 * k for k in range(2, far)]),
        shape((blks, cands, nq), F32),
        (own, *pieces, *distant),
        name="near",
    )
    line = (owned, total_q + 128)
    sums = small(
        functools.partial(scores_kernel, (blks, groups)),
        [shape(line, F32)] * groups,
        (own, squares, near, late, passed),
        [pltpu.VMEM((blks, cands, nq), F32), pltpu.VMEM((groups,) + line, F32)],
        name="scores",
    )
    return small(
        functools.partial(finish_kernel, pdim),
        shape((owned, total_q), F32),
        (sums[0], *[grp_swap(sums[k], k) for k in range(1, groups)]),
        name="finish",
    )


def solution(mesh):
    in_specs = (
        P(None, "blk", "grp", None),
        P(None, "blk", "grp", None),
        P(),
        P(),
        P("blk"),
        P("blk", None),
    )
    return jax.shard_map(
        functools.partial(on_device, mesh.shape["blk"], mesh.shape["grp"]),
        mesh=mesh,
        in_specs=in_specs,
        out_specs=P(("blk", "grp"), None),
        check_vma=False,
    )
```

```python
import functools

import jax
import jax.numpy as jnp
from jax import lax
from jax.experimental import pallas as pl
from jax.experimental.pallas import tpu as pltpu
from jax.sharding import PartitionSpec as P

EPS = 1e-06
GRANT = 54784
F32 = jnp.float32
BF16 = jnp.bfloat16
VMEM = pl.BlockSpec(memory_space=pltpu.VMEM)
ANY = pl.BlockSpec(memory_space=pl.ANY)
BY_ROWS = (((1,), (1,)), ((), ()))


def grads_kernel(dims, lens_in, acts, grads, w_in, w_out, send, keep, *scratch):
    cands, tokens, width, groups = dims
    act_buf, grad_buf, win_raw, wout_raw, win, wout, lens, store, sems, wsems = scratch
    chunks = cands // 4
    rows = 4 * tokens
    loads = []
    for side, (source, buf) in enumerate(((grads, grad_buf), (acts, act_buf))):
        for i in range(chunks):
            parts = [pl.ds((2 * i + h) * (rows // 2), rows // 2) for h in range(2)]
            loads.append(
                [
                    pltpu.make_async_copy(source.at[part], buf.at[part], sems.at[side, 2 * i + h])
                    for h, part in enumerate(parts)
                ]
            )

    def start(n):
        if n < len(loads):
            for load in loads[n]:
                load.start()

    def wait(n):
        for load in loads[n]:
            load.wait()

    load_lens = pltpu.make_async_copy(lens_in, lens, wsems.at[2])
    load_wout = pltpu.make_async_copy(w_out, wout_raw, wsems.at[0])
    load_win = pltpu.make_async_copy(w_in, win_raw, wsems.at[1])
    load_wout.start()
    load_win.start()
    load_lens.start()
    for n in range(3):
        start(n)
    grp = lax.axis_index("grp")
    lines = width // groups
    position = lax.broadcasted_iota(jnp.int32, (tokens, width), 0) + grp * tokens
    row_blk = lax.broadcasted_iota(jnp.int32, (rows, rows), 0) // tokens
    col_blk = lax.broadcasted_iota(jnp.int32, (rows, 4 * width), 1) // width
    diagonal = row_blk == col_blk // 2 + 2 * (col_blk % 2)

    def add_up(i, left, xp):
        used = []
        for j in range(4):
            used.append(jnp.where(position < lens[4 * i + j], xp[j * tokens : (j + 1) * tokens], 0.0))
        wide = jnp.concatenate([jnp.concatenate(used, axis=0)] * 4, axis=1)
        right = jnp.where(diagonal, wide, 0.0).astype(BF16)
        sums = jnp.dot(left, right, preferred_element_type=F32)
        for t in range(2):
            there = slice((2 * i + t) * lines, (2 * i + t + 1) * lines)
            for s in range(groups):
                store[s, there, :] = sums[s * lines : (s + 1) * lines, t * 128 : (t + 1) * 128]

    load_wout.wait()
    wout[...] = wout_raw[...].T
    load_win.wait()
    load_lens.wait()
    lefts = []
    for i in range(chunks):
        wait(i)
        start(i + 3)
        part = pl.ds(i * rows, rows)
        gp = jnp.dot(grad_buf[part, :], wout[...], preferred_element_type=F32)
        if i == 0:
            win[...] = win_raw[...].T
        lefts.append(gp.T.astype(BF16))
    pending = None
    for i in range(chunks):
        if i < chunks - 1:
            wait(chunks + i)
            start(chunks + i + 3)
            part = pl.ds(i * rows, rows)
            xp = jnp.dot(act_buf[part, :], win[...], preferred_element_type=F32)
        else:
            pieces = []
            for h, load in enumerate(loads[chunks + i]):
                load.wait()
                piece = pl.ds(i * rows + h * (rows // 2), rows // 2)
                pieces.append(jnp.dot(act_buf[piece, :], win[...], preferred_element_type=F32))
            xp = jnp.concatenate(pieces, axis=0)
        if pending is not None:
            add_up(*pending)
        pending = (i, lefts[i], xp)
    add_up(*pending)
    core = lax.rem(grp, 2)
    for x in range(groups // 2):
        send[x] = store[2 * x + 1 - core]
        keep[x] = store[2 * x + core]


def fold_kernel(keep, came, *rest):
    send, kept = rest[-2:]
    x = lax.axis_index("grp") // 2
    send[...] = (keep[1 - x] + came[1 - x]).astype(BF16)
    kept[...] = keep[x] + came[x]


def combine_kernel(dims, kept, came, *rest):
    half, lines, width = dims
    out, squares, grads = rest[-3:]
    grads[...] = kept[...] + came[...].astype(F32)
    low = lax.broadcasted_iota(jnp.int32, (half, 128), 1) < width
    sums, columns = None, []
    for e in range(0, lines, 2):
        first = grads[pl.ds(e, half, stride=lines), :]
        second = grads[pl.ds(e + 1, half, stride=lines), :]
        line = jnp.concatenate(
            [
                jnp.where(low, first, pltpu.roll(second, width, 1)),
                jnp.where(low, pltpu.roll(first, width, 1), second),
            ],
            axis=0,
        )
        columns.append(line.astype(BF16))
        sums = line * line if sums is None else sums + line * line
    squares[...] = sums
    out[...] = jnp.concatenate(columns, axis=1)


def join_kernel(count, *refs):
    out = refs[-1]
    nq = refs[-2].shape[0]
    for n, ref in enumerate(refs[-1 - count : -1]):
        out[n * nq : (n + 1) * nq, :] = ref[...]


def near_kernel(dims, left, *refs):
    blk = lax.axis_index("blk")
    place = refs[-1]
    for flip, piece in zip(dims, refs[:-1]):
        place[jnp.bitwise_xor(blk, flip)] = lax.dot_general(
            left[...], piece[...], BY_ROWS, preferred_element_type=F32
        )


def late_kernel(left, queries, out):
    out[...] = lax.dot_general(left[...], queries[...], BY_ROWS, preferred_element_type=F32)


def scores_kernel(dims, left, squares, near, late, passed, *rest):
    blks, groups = dims
    outs = rest[:groups]
    place, result = rest[groups:]
    rows = left[...]
    blk = lax.axis_index("blk")
    nq = near.shape[2]
    place[...] = near[...]
    place[jnp.bitwise_xor(blk, 2)] = late[...]
    handed = lax.dot_general(rows, passed[...], BY_ROWS, preferred_element_type=F32)
    for n in range(blks // 2 - 2):
        place[jnp.bitwise_xor(blk, 2 * n + 5)] = handed[:, n * nq : (n + 1) * nq]
    scores = jnp.concatenate([place[b] for b in range(blks)], axis=1)
    width = blks * nq
    half = scores.shape[0] // 2
    owned = half // groups
    for g in range(groups):
        for h in range(2):
            here = slice(h * half + g * owned, h * half + (g + 1) * owned)
            there = slice(h * owned, (h + 1) * owned)
            result[g, there, :width] = scores[here]
            result[g, there, width:] = squares[here, :]
    grp = lax.axis_index("grp")
    for k in range(groups):
        outs[k][...] = result[jnp.bitwise_xor(grp, k)]


def finish_kernel(pdim, *refs):
    out = refs[-1]
    total = refs[0][...]
    for ref in refs[1:-1]:
        total = total + ref[...]
    width = out.shape[1]
    mean = jnp.sum(total[:, width:], axis=1, keepdims=True) / pdim
    out[...] = total[:, :width] * lax.rsqrt(mean + EPS)


def small(kernel, out_shape, operands, scratch_shapes=(), name=None):
    one = not isinstance(out_shape, list)
    return pl.pallas_call(
        kernel,
        out_shape=out_shape,
        in_specs=[VMEM] * len(operands),
        out_specs=VMEM if one else [VMEM] * len(out_shape),
        scratch_shapes=list(scratch_shapes),
        compiler_params=pltpu.CompilerParams(vmem_limit_bytes=16 * 2**20),
        name=name,
    )(*operands)


def on_device(blks, groups, acts, out_grads, proj_in, proj_out, lengths, queries):
    _, cands, tokens, depth = acts.shape
    width = proj_in.shape[2]
    far = blks // 2
    pdim = width * width
    lines = width // groups
    nq = queries.shape[0]
    total_q = nq * blks
    owned = cands // groups
    slice_width = pdim // groups
    shape = jax.ShapeDtypeStruct

    def grp_swap(x, k):
        return lax.ppermute(x, "grp", [(g, g ^ k) for g in range(groups)])

    def blk_swap(x, k):
        return lax.ppermute(x, "blk", [(b, b ^ k) for b in range(blks)])

    cut = lax.dynamic_slice(queries, (0, lax.axis_index("grp") * slice_width), (nq, slice_width))
    cut, lens = lax.optimization_barrier((cut, jnp.minimum(lengths, tokens * groups)))
    pieces = [cut, blk_swap(cut, 1), blk_swap(cut, 3)]
    distant = [blk_swap(cut, 2 * k) for k in range(2, far)]

    rows = cands * tokens
    piece = (cands // 2 * lines, 128)
    send, keep = pl.pallas_call(
        functools.partial(grads_kernel, (cands, tokens, width, groups)),
        out_shape=[shape((groups // 2,) + piece, F32)] * 2,
        in_specs=[ANY] * 5,
        out_specs=[VMEM] * 2,
        scratch_shapes=[
            pltpu.VMEM((rows, depth), BF16),
            pltpu.VMEM((rows, depth), BF16),
            pltpu.VMEM((width, depth), BF16),
            pltpu.VMEM((width, depth), BF16),
            pltpu.VMEM((depth, width), BF16),
            pltpu.VMEM((depth, width), BF16),
            pltpu.SMEM((cands,), jnp.int32),
            pltpu.VMEM((groups,) + piece, F32),
            pltpu.SemaphoreType.DMA((2, cands // 2)),
            pltpu.SemaphoreType.DMA((3,)),
        ],
        compiler_params=pltpu.CompilerParams(vmem_limit_bytes=GRANT * 2**10),
        cost_estimate=pl.CostEstimate(
            flops=16 * rows * depth * width, bytes_accessed=4 * rows * depth, transcendentals=0
        ),
        name="grads",
    )(
        lens,
        acts.reshape(rows, depth),
        out_grads.reshape(rows, depth),
        proj_in[0].T,
        proj_out[0].T,
    )
    joined = small(
        functools.partial(join_kernel, far - 2),
        shape(((far - 2) * nq, slice_width), BF16),
        (*pieces[1:], keep, *distant),
        name="join",
    )
    late, joined = lax.optimization_barrier((cut, joined))
    late = blk_swap(late, 2)
    send, kept = small(
        fold_kernel,
        [shape(piece, BF16), shape(piece, F32)],
        (keep, grp_swap(send, 1), joined),
        name="fold",
    )
    passed = blk_swap(joined, 1)
    own, squares = small(
        functools.partial(combine_kernel, (cands // 2, lines, width)),
        [shape((cands, slice_width), BF16), shape((cands, 128), F32)],
        (kept, grp_swap(send, 2)),
        [pltpu.VMEM(piece, F32)],
        name="combine",
    )
    near = small(
        functools.partial(near_kernel, [0, 1, 3] + [2 * k for k in range(2, far)]),
        shape((blks, cands, nq), F32),
        (own, *pieces, *distant),
        name="near",
    )
    late = small(late_kernel, shape((cands, nq), F32), (own, late), name="late")
    line = (owned, total_q + 128)
    sums = small(
        functools.partial(scores_kernel, (blks, groups)),
        [shape(line, F32)] * groups,
        (own, squares, near, late, passed),
        [pltpu.VMEM((blks, cands, nq), F32), pltpu.VMEM((groups,) + line, F32)],
        name="scores",
    )
    return small(
        functools.partial(finish_kernel, pdim),
        shape((owned, total_q), F32),
        (sums[0], *[grp_swap(sums[k], k) for k in range(1, groups)]),
        name="finish",
    )


def solution(mesh):
    in_specs = (
        P(None, "blk", "grp", None),
        P(None, "blk", "grp", None),
        P(),
        P(),
        P("blk"),
        P("blk", None),
    )
    return jax.shard_map(
        functools.partial(on_device, mesh.shape["blk"], mesh.shape["grp"]),
        mesh=mesh,
        in_specs=in_specs,
        out_specs=P(("blk", "grp"), None),
        check_vma=False,
    )
```

```python
import functools

import jax
import jax.numpy as jnp
from jax import lax
from jax.experimental import pallas as pl
from jax.experimental.pallas import tpu as pltpu
from jax.sharding import PartitionSpec as P

EPS = 1e-06
GRANT = 54784
F32 = jnp.float32
BF16 = jnp.bfloat16
VMEM = pl.BlockSpec(memory_space=pltpu.VMEM)
ANY = pl.BlockSpec(memory_space=pl.ANY)
BY_ROWS = (((1,), (1,)), ((), ()))


def grads_kernel(dims, lens_in, acts, grads, w_in, w_out, send, keep, *scratch):
    cands, tokens, width, groups = dims
    act_buf, grad_buf, win_raw, wout_raw, win, wout, lens, store, sems, wsems = scratch
    chunks = cands // 4
    rows = 4 * tokens
    loads = []
    for i in range(chunks):
        for side, (source, buf) in enumerate(((grads, grad_buf), (acts, act_buf))):
            parts = [pl.ds((2 * i + h) * (rows // 2), rows // 2) for h in range(2)]
            loads.append(
                [
                    pltpu.make_async_copy(source.at[part], buf.at[part], sems.at[side, 2 * i + h])
                    for h, part in enumerate(parts)
                ]
            )

    def start(n):
        if n < len(loads):
            for load in loads[n]:
                load.start()

    def wait(n):
        for load in loads[n]:
            load.wait()

    load_lens = pltpu.make_async_copy(lens_in, lens, wsems.at[2])
    load_wout = pltpu.make_async_copy(w_out, wout_raw, wsems.at[0])
    load_win = pltpu.make_async_copy(w_in, win_raw, wsems.at[1])
    load_wout.start()
    load_win.start()
    load_lens.start()
    for n in range(3):
        start(n)
    grp = lax.axis_index("grp")
    lines = width // groups
    position = lax.broadcasted_iota(jnp.int32, (tokens, width), 0) + grp * tokens
    row_blk = lax.broadcasted_iota(jnp.int32, (rows, rows), 0) // tokens
    col_blk = lax.broadcasted_iota(jnp.int32, (rows, 4 * width), 1) // width
    diagonal = row_blk == col_blk // 2 + 2 * (col_blk % 2)

    def add_up(i, left, xp):
        used = []
        for j in range(4):
            used.append(jnp.where(position < lens[4 * i + j], xp[j * tokens : (j + 1) * tokens], 0.0))
        wide = jnp.concatenate([jnp.concatenate(used, axis=0)] * 4, axis=1)
        right = jnp.where(diagonal, wide, 0.0).astype(BF16)
        sums = jnp.dot(left, right, preferred_element_type=F32)
        for t in range(2):
            there = slice((2 * i + t) * lines, (2 * i + t + 1) * lines)
            for s in range(groups):
                store[s, there, :] = sums[s * lines : (s + 1) * lines, t * 128 : (t + 1) * 128]

    load_wout.wait()
    wout[...] = wout_raw[...].T
    load_win.wait()
    load_lens.wait()
    pending = None
    for i in range(chunks):
        part = pl.ds(i * rows, rows)
        wait(2 * i)
        start(2 * i + 3)
        gp = jnp.dot(grad_buf[part, :], wout[...], preferred_element_type=F32)
        if i == 0:
            win[...] = win_raw[...].T
        else:
            add_up(*pending)
        left = gp.T.astype(BF16)
        if i < chunks - 1:
            wait(2 * i + 1)
            start(2 * i + 4)
            xp = jnp.dot(act_buf[part, :], win[...], preferred_element_type=F32)
        else:
            pieces = []
            for h, load in enumerate(loads[2 * i + 1]):
                load.wait()
                piece = pl.ds(i * rows + h * (rows // 2), rows // 2)
                pieces.append(jnp.dot(act_buf[piece, :], win[...], preferred_element_type=F32))
            xp = jnp.concatenate(pieces, axis=0)
        pending = (i, left, xp)
    add_up(*pending)
    core = lax.rem(grp, 2)
    for x in range(groups // 2):
        send[x] = store[2 * x + 1 - core]
        keep[x] = store[2 * x + core]


def fold_kernel(keep, came, *rest):
    send, kept = rest[-2:]
    x = lax.axis_index("grp") // 2
    send[...] = (keep[1 - x] + came[1 - x]).astype(BF16)
    kept[...] = keep[x] + came[x]


def combine_kernel(dims, kept, came, *rest):
    half, lines, width = dims
    out, squares, grads = rest[-3:]
    grads[...] = kept[...] + came[...].astype(F32)
    low = lax.broadcasted_iota(jnp.int32, (half, 128), 1) < width
    sums, columns = None, []
    for e in range(0, lines, 2):
        first = grads[pl.ds(e, half, stride=lines), :]
        second = grads[pl.ds(e + 1, half, stride=lines), :]
        line = jnp.concatenate(
            [
                jnp.where(low, first, pltpu.roll(second, width, 1)),
                jnp.where(low, pltpu.roll(first, width, 1), second),
            ],
            axis=0,
        )
        columns.append(line.astype(BF16))
        sums = line * line if sums is None else sums + line * line
    squares[...] = sums
    out[...] = jnp.concatenate(columns, axis=1)


def join_kernel(count, *refs):
    out = refs[-1]
    nq = refs[-2].shape[0]
    for n, ref in enumerate(refs[-1 - count : -1]):
        out[n * nq : (n + 1) * nq, :] = ref[...]


def near_kernel(dims, left, *refs):
    blk = lax.axis_index("blk")
    place = refs[-1]
    for flip, piece in zip(dims, refs[:-1]):
        place[jnp.bitwise_xor(blk, flip)] = lax.dot_general(
            left[...], piece[...], BY_ROWS, preferred_element_type=F32
        )


def scores_kernel(dims, left, squares, near, late, passed, *rest):
    blks, groups = dims
    outs = rest[:groups]
    place, result = rest[groups:]
    rows = left[...]
    blk = lax.axis_index("blk")
    nq = near.shape[2]
    place[...] = near[...]
    place[jnp.bitwise_xor(blk, 2)] = lax.dot_general(
        rows, late[...], BY_ROWS, preferred_element_type=F32
    )
    for n in range(blks // 2 - 2):
        place[jnp.bitwise_xor(blk, 2 * n + 5)] = lax.dot_general(
            rows, passed[n * nq : (n + 1) * nq, :], BY_ROWS, preferred_element_type=F32
        )
    scores = jnp.concatenate([place[b] for b in range(blks)], axis=1)
    width = blks * nq
    half = scores.shape[0] // 2
    owned = half // groups
    for g in range(groups):
        for h in range(2):
            here = slice(h * half + g * owned, h * half + (g + 1) * owned)
            there = slice(h * owned, (h + 1) * owned)
            result[g, there, :width] = scores[here]
            result[g, there, width:] = squares[here, :]
    grp = lax.axis_index("grp")
    for k in range(groups):
        outs[k][...] = result[jnp.bitwise_xor(grp, k)]


def finish_kernel(pdim, *refs):
    out = refs[-1]
    total = refs[0][...]
    for ref in refs[1:-1]:
        total = total + ref[...]
    width = out.shape[1]
    mean = jnp.sum(total[:, width:], axis=1, keepdims=True) / pdim
    out[...] = total[:, :width] * lax.rsqrt(mean + EPS)


def small(kernel, out_shape, operands, scratch_shapes=(), name=None):
    one = not isinstance(out_shape, list)
    return pl.pallas_call(
        kernel,
        out_shape=out_shape,
        in_specs=[VMEM] * len(operands),
        out_specs=VMEM if one else [VMEM] * len(out_shape),
        scratch_shapes=list(scratch_shapes),
        compiler_params=pltpu.CompilerParams(vmem_limit_bytes=16 * 2**20),
        name=name,
    )(*operands)


def on_device(blks, groups, acts, out_grads, proj_in, proj_out, lengths, queries):
    _, cands, tokens, depth = acts.shape
    width = proj_in.shape[2]
    far = blks // 2
    pdim = width * width
    lines = width // groups
    nq = queries.shape[0]
    total_q = nq * blks
    owned = cands // groups
    slice_width = pdim // groups
    shape = jax.ShapeDtypeStruct

    def grp_swap(x, k):
        return lax.ppermute(x, "grp", [(g, g ^ k) for g in range(groups)])

    def blk_swap(x, k):
        return lax.ppermute(x, "blk", [(b, b ^ k) for b in range(blks)])

    cut = lax.dynamic_slice(queries, (0, lax.axis_index("grp") * slice_width), (nq, slice_width))
    cut, lens = lax.optimization_barrier((cut, jnp.minimum(lengths, tokens * groups)))
    pieces = [cut, blk_swap(cut, 1), blk_swap(cut, 3)]
    distant = [blk_swap(cut, 2 * k) for k in range(2, far)]

    rows = cands * tokens
    piece = (cands // 2 * lines, 128)
    send, keep = pl.pallas_call(
        functools.partial(grads_kernel, (cands, tokens, width, groups)),
        out_shape=[shape((groups // 2,) + piece, F32)] * 2,
        in_specs=[ANY] * 5,
        out_specs=[VMEM] * 2,
        scratch_shapes=[
            pltpu.VMEM((rows, depth), BF16),
            pltpu.VMEM((rows, depth), BF16),
            pltpu.VMEM((width, depth), BF16),
            pltpu.VMEM((width, depth), BF16),
            pltpu.VMEM((depth, width), BF16),
            pltpu.VMEM((depth, width), BF16),
            pltpu.SMEM((cands,), jnp.int32),
            pltpu.VMEM((groups,) + piece, F32),
            pltpu.SemaphoreType.DMA((2, cands // 2)),
            pltpu.SemaphoreType.DMA((3,)),
        ],
        compiler_params=pltpu.CompilerParams(vmem_limit_bytes=GRANT * 2**10),
        cost_estimate=pl.CostEstimate(
            flops=16 * rows * depth * width, bytes_accessed=4 * rows * depth, transcendentals=0
        ),
        name="grads",
    )(
        lens,
        acts.reshape(rows, depth),
        out_grads.reshape(rows, depth),
        proj_in[0].T,
        proj_out[0].T,
    )
    joined = small(
        functools.partial(join_kernel, far - 2),
        shape(((far - 2) * nq, slice_width), BF16),
        (*pieces[1:], keep, *distant),
        name="join",
    )
    late, joined = lax.optimization_barrier((cut, joined))
    late = blk_swap(late, 2)
    send, kept = small(
        fold_kernel,
        [shape(piece, BF16), shape(piece, F32)],
        (keep, grp_swap(send, 1), joined),
        name="fold",
    )
    passed = blk_swap(joined, 1)
    own, squares = small(
        functools.partial(combine_kernel, (cands // 2, lines, width)),
        [shape((cands, slice_width), BF16), shape((cands, 128), F32)],
        (kept, grp_swap(send, 2)),
        [pltpu.VMEM(piece, F32)],
        name="combine",
    )
    near = small(
        functools.partial(near_kernel, [0, 1, 3] + [2 * k for k in range(2, far)]),
        shape((blks, cands, nq), F32),
        (own, *pieces, *distant),
        name="near",
    )
    line = (owned, total_q + 128)
    sums = small(
        functools.partial(scores_kernel, (blks, groups)),
        [shape(line, F32)] * groups,
        (own, squares, near, late, passed),
        [pltpu.VMEM((blks, cands, nq), F32), pltpu.VMEM((groups,) + line, F32)],
        name="scores",
    )
    return small(
        functools.partial(finish_kernel, pdim),
        shape((owned, total_q), F32),
        (sums[0], *[grp_swap(sums[k], k) for k in range(groups - 1, 0, -1)]),
        name="finish",
    )


def solution(mesh):
    in_specs = (
        P(None, "blk", "grp", None),
        P(None, "blk", "grp", None),
        P(),
        P(),
        P("blk"),
        P("blk", None),
    )
    return jax.shard_map(
        functools.partial(on_device, mesh.shape["blk"], mesh.shape["grp"]),
        mesh=mesh,
        in_specs=in_specs,
        out_specs=P(("blk", "grp"), None),
        check_vma=False,
    )
```

```python
import functools

import jax
import jax.numpy as jnp
from jax import lax
from jax.experimental import pallas as pl
from jax.experimental.pallas import tpu as pltpu
from jax.sharding import PartitionSpec as P

EPS = 1e-06
GRANT = 54784
F32 = jnp.float32
BF16 = jnp.bfloat16
VMEM = pl.BlockSpec(memory_space=pltpu.VMEM)
ANY = pl.BlockSpec(memory_space=pl.ANY)
BY_ROWS = (((1,), (1,)), ((), ()))


def grads_kernel(dims, lens_in, acts, grads, w_in, w_out, send, keep, *scratch):
    cands, tokens, width, groups = dims
    act_buf, grad_buf, win_raw, wout_raw, win, wout, lens, store, sems, wsems = scratch
    chunks = cands // 4
    rows = 4 * tokens
    loads = []
    for i in range(chunks):
        for side, (source, buf) in enumerate(((grads, grad_buf), (acts, act_buf))):
            parts = [pl.ds((2 * i + h) * (rows // 2), rows // 2) for h in range(2)]
            loads.append(
                [
                    pltpu.make_async_copy(source.at[part], buf.at[part], sems.at[side, 2 * i + h])
                    for h, part in enumerate(parts)
                ]
            )

    def start(n):
        if n < len(loads):
            for load in loads[n]:
                load.start()

    def wait(n):
        for load in loads[n]:
            load.wait()

    load_lens = pltpu.make_async_copy(lens_in, lens, wsems.at[2])
    load_wout = pltpu.make_async_copy(w_out, wout_raw, wsems.at[0])
    load_win = pltpu.make_async_copy(w_in, win_raw, wsems.at[1])
    load_wout.start()
    load_win.start()
    load_lens.start()
    for n in range(3):
        start(n)
    grp = lax.axis_index("grp")
    lines = width // groups
    position = lax.broadcasted_iota(jnp.int32, (tokens, width), 0) + grp * tokens
    row_blk = lax.broadcasted_iota(jnp.int32, (rows, rows), 0) // tokens
    col_blk = lax.broadcasted_iota(jnp.int32, (rows, 4 * width), 1) // width
    diagonal = row_blk == col_blk // 2 + 2 * (col_blk % 2)

    def add_up(i, left, xp):
        used = []
        for j in range(4):
            used.append(jnp.where(position < lens[4 * i + j], xp[j * tokens : (j + 1) * tokens], 0.0))
        wide = jnp.concatenate([jnp.concatenate(used, axis=0)] * 4, axis=1)
        right = jnp.where(diagonal, wide, 0.0).astype(BF16)
        sums = jnp.dot(left, right, preferred_element_type=F32)
        for t in range(2):
            there = slice((2 * i + t) * lines, (2 * i + t + 1) * lines)
            for s in range(groups):
                store[s, there, :] = sums[s * lines : (s + 1) * lines, t * 128 : (t + 1) * 128]

    load_wout.wait()
    wout[...] = wout_raw[...].T
    load_win.wait()
    load_lens.wait()
    pending = None
    for i in range(chunks):
        part = pl.ds(i * rows, rows)
        wait(2 * i)
        start(2 * i + 3)
        gp = jnp.dot(grad_buf[part, :], wout[...], preferred_element_type=F32)
        if i == 0:
            win[...] = win_raw[...].T
        else:
            add_up(*pending)
        left = gp.T.astype(BF16)
        if i < chunks - 1:
            wait(2 * i + 1)
            start(2 * i + 4)
            xp = jnp.dot(act_buf[part, :], win[...], preferred_element_type=F32)
        else:
            pieces = []
            for h, load in enumerate(loads[2 * i + 1]):
                load.wait()
                piece = pl.ds(i * rows + h * (rows // 2), rows // 2)
                pieces.append(jnp.dot(act_buf[piece, :], win[...], preferred_element_type=F32))
            xp = jnp.concatenate(pieces, axis=0)
        pending = (i, left, xp)
    add_up(*pending)
    core = lax.rem(grp, 2)
    for x in range(groups // 2):
        send[x] = store[2 * x + 1 - core]
        keep[x] = store[2 * x + core]


def fold_kernel(keep, came, *rest):
    send, kept = rest[-2:]
    x = lax.axis_index("grp") // 2
    send[...] = (keep[1 - x] + came[1 - x]).astype(BF16)
    kept[...] = keep[x] + came[x]


def combine_kernel(dims, kept, came, *rest):
    half, lines, width = dims
    out, squares, grads = rest[-3:]
    grads[...] = kept[...] + came[...].astype(F32)
    low = lax.broadcasted_iota(jnp.int32, (half, 128), 1) < width
    sums, columns = None, []
    for e in range(0, lines, 2):
        first = grads[pl.ds(e, half, stride=lines), :]
        second = grads[pl.ds(e + 1, half, stride=lines), :]
        line = jnp.concatenate(
            [
                jnp.where(low, first, pltpu.roll(second, width, 1)),
                jnp.where(low, pltpu.roll(first, width, 1), second),
            ],
            axis=0,
        )
        columns.append(line.astype(BF16))
        sums = line * line if sums is None else sums + line * line
    squares[...] = sums
    out[...] = jnp.concatenate(columns, axis=1)


def join_kernel(count, *refs):
    out = refs[-1]
    nq = refs[-2].shape[0]
    for n, ref in enumerate(refs[-1 - count : -1]):
        out[n * nq : (n + 1) * nq, :] = ref[...]


def near_kernel(dims, left, *refs):
    blk = lax.axis_index("blk")
    place = refs[-1]
    for flip, piece in zip(dims, refs[:-1]):
        place[jnp.bitwise_xor(blk, flip)] = lax.dot_general(
            left[...], piece[...], BY_ROWS, preferred_element_type=F32
        )


def scores_kernel(dims, left, squares, near, late, passed, *rest):
    blks, groups = dims
    outs = rest[:groups]
    place, result = rest[groups:]
    rows = left[...]
    blk = lax.axis_index("blk")
    nq = near.shape[2]
    place[...] = near[...]
    place[jnp.bitwise_xor(blk, 2)] = lax.dot_general(
        rows, late[...], BY_ROWS, preferred_element_type=F32
    )
    for n in range(blks // 2 - 2):
        place[jnp.bitwise_xor(blk, 2 * n + 5)] = lax.dot_general(
            rows, passed[n * nq : (n + 1) * nq, :], BY_ROWS, preferred_element_type=F32
        )
    scores = jnp.concatenate([place[b] for b in range(blks)], axis=1)
    width = blks * nq
    half = scores.shape[0] // 2
    owned = half // groups
    for g in range(groups):
        for h in range(2):
            here = slice(h * half + g * owned, h * half + (g + 1) * owned)
            there = slice(h * owned, (h + 1) * owned)
            result[g, there, :width] = scores[here]
            result[g, there, width:] = squares[here, :]
    grp = lax.axis_index("grp")
    for k in range(groups):
        outs[k][...] = result[jnp.bitwise_xor(grp, k)]


def small(kernel, out_shape, operands, scratch_shapes=(), name=None):
    one = not isinstance(out_shape, list)
    return pl.pallas_call(
        kernel,
        out_shape=out_shape,
        in_specs=[VMEM] * len(operands),
        out_specs=VMEM if one else [VMEM] * len(out_shape),
        scratch_shapes=list(scratch_shapes),
        compiler_params=pltpu.CompilerParams(vmem_limit_bytes=16 * 2**20),
        name=name,
    )(*operands)


def on_device(blks, groups, acts, out_grads, proj_in, proj_out, lengths, queries):
    _, cands, tokens, depth = acts.shape
    width = proj_in.shape[2]
    far = blks // 2
    pdim = width * width
    lines = width // groups
    nq = queries.shape[0]
    total_q = nq * blks
    owned = cands // groups
    slice_width = pdim // groups
    shape = jax.ShapeDtypeStruct

    def grp_swap(x, k):
        return lax.ppermute(x, "grp", [(g, g ^ k) for g in range(groups)])

    def blk_swap(x, k):
        return lax.ppermute(x, "blk", [(b, b ^ k) for b in range(blks)])

    cut = lax.dynamic_slice(queries, (0, lax.axis_index("grp") * slice_width), (nq, slice_width))
    cut, lens = lax.optimization_barrier((cut, jnp.minimum(lengths, tokens * groups)))
    pieces = [cut, blk_swap(cut, 1), blk_swap(cut, 3)]
    distant = [blk_swap(cut, 2 * k) for k in range(2, far)]

    rows = cands * tokens
    piece = (cands // 2 * lines, 128)
    send, keep = pl.pallas_call(
        functools.partial(grads_kernel, (cands, tokens, width, groups)),
        out_shape=[shape((groups // 2,) + piece, F32)] * 2,
        in_specs=[ANY] * 5,
        out_specs=[VMEM] * 2,
        scratch_shapes=[
            pltpu.VMEM((rows, depth), BF16),
            pltpu.VMEM((rows, depth), BF16),
            pltpu.VMEM((width, depth), BF16),
            pltpu.VMEM((width, depth), BF16),
            pltpu.VMEM((depth, width), BF16),
            pltpu.VMEM((depth, width), BF16),
            pltpu.SMEM((cands,), jnp.int32),
            pltpu.VMEM((groups,) + piece, F32),
            pltpu.SemaphoreType.DMA((2, cands // 2)),
            pltpu.SemaphoreType.DMA((3,)),
        ],
        compiler_params=pltpu.CompilerParams(vmem_limit_bytes=GRANT * 2**10),
        cost_estimate=pl.CostEstimate(
            flops=16 * rows * depth * width, bytes_accessed=4 * rows * depth, transcendentals=0
        ),
        name="grads",
    )(
        lens,
        acts.reshape(rows, depth),
        out_grads.reshape(rows, depth),
        proj_in[0].T,
        proj_out[0].T,
    )
    joined = small(
        functools.partial(join_kernel, far - 2),
        shape(((far - 2) * nq, slice_width), BF16),
        (*pieces[1:], keep, *distant),
        name="join",
    )
    late, joined = lax.optimization_barrier((cut, joined))
    late = blk_swap(late, 2)
    send, kept = small(
        fold_kernel,
        [shape(piece, BF16), shape(piece, F32)],
        (keep, grp_swap(send, 1), joined),
        name="fold",
    )
    passed = blk_swap(joined, 1)
    own, squares = small(
        functools.partial(combine_kernel, (cands // 2, lines, width)),
        [shape((cands, slice_width), BF16), shape((cands, 128), F32)],
        (kept, grp_swap(send, 2)),
        [pltpu.VMEM(piece, F32)],
        name="combine",
    )
    near = small(
        functools.partial(near_kernel, [0, 1, 3] + [2 * k for k in range(2, far)]),
        shape((blks, cands, nq), F32),
        (own, *pieces, *distant),
        name="near",
    )
    line = (owned, total_q + 128)
    sums = small(
        functools.partial(scores_kernel, (blks, groups)),
        [shape(line, F32)] * groups,
        (own, squares, near, late, passed),
        [pltpu.VMEM((blks, cands, nq), F32), pltpu.VMEM((groups,) + line, F32)],
        name="scores",
    )
    total = sums[0]
    for k in range(groups - 1, 0, -1):
        total = total + grp_swap(sums[k], k)
    mean = jnp.sum(total[:, total_q:], axis=1, keepdims=True) / pdim
    return total[:, :total_q] * lax.rsqrt(mean + EPS)


def solution(mesh):
    in_specs = (
        P(None, "blk", "grp", None),
        P(None, "blk", "grp", None),
        P(),
        P(),
        P("blk"),
        P("blk", None),
    )
    return jax.shard_map(
        functools.partial(on_device, mesh.shape["blk"], mesh.shape["grp"]),
        mesh=mesh,
        in_specs=in_specs,
        out_specs=P(("blk", "grp"), None),
        check_vma=False,
    )
```

```python
import functools

import jax
import jax.numpy as jnp
from jax import lax
from jax.experimental import pallas as pl
from jax.experimental.pallas import tpu as pltpu
from jax.sharding import PartitionSpec as P

EPS = 1e-06
GRANT = 54784
F32 = jnp.float32
BF16 = jnp.bfloat16
VMEM = pl.BlockSpec(memory_space=pltpu.VMEM)
ANY = pl.BlockSpec(memory_space=pl.ANY)
BY_ROWS = (((1,), (1,)), ((), ()))


def grads_kernel(dims, lens_in, acts, grads, w_in, w_out, send, keep, *scratch):
    cands, tokens, width, groups = dims
    act_buf, grad_buf, win_raw, wout_raw, win, wout, lens, store, sems, wsems = scratch
    chunks = cands // 4
    rows = 4 * tokens
    loads = []
    for i in range(chunks):
        for side, (source, buf) in enumerate(((grads, grad_buf), (acts, act_buf))):
            parts = [pl.ds((2 * i + h) * (rows // 2), rows // 2) for h in range(2)]
            loads.append(
                [
                    pltpu.make_async_copy(source.at[part], buf.at[part], sems.at[side, 2 * i + h])
                    for h, part in enumerate(parts)
                ]
            )

    def start(n):
        if n < len(loads):
            for load in loads[n]:
                load.start()

    def wait(n):
        for load in loads[n]:
            load.wait()

    load_lens = pltpu.make_async_copy(lens_in, lens, wsems.at[2])
    load_wout = pltpu.make_async_copy(w_out, wout_raw, wsems.at[0])
    load_win = pltpu.make_async_copy(w_in, win_raw, wsems.at[1])
    load_wout.start()
    load_win.start()
    load_lens.start()
    for n in range(3):
        start(n)
    grp = lax.axis_index("grp")
    lines = width // groups
    position = lax.broadcasted_iota(jnp.int32, (tokens, width), 0) + grp * tokens
    row_blk = lax.broadcasted_iota(jnp.int32, (rows, rows), 0) // tokens
    col_blk = lax.broadcasted_iota(jnp.int32, (rows, 4 * width), 1) // width
    diagonal = row_blk == col_blk // 2 + 2 * (col_blk % 2)

    def add_up(i, left, xp):
        used = []
        for j in range(4):
            used.append(jnp.where(position < lens[4 * i + j], xp[j * tokens : (j + 1) * tokens], 0.0))
        wide = jnp.concatenate([jnp.concatenate(used, axis=0)] * 4, axis=1)
        right = jnp.where(diagonal, wide, 0.0).astype(BF16)
        sums = jnp.dot(left, right, preferred_element_type=F32)
        for t in range(2):
            there = slice((2 * i + t) * lines, (2 * i + t + 1) * lines)
            for s in range(groups):
                store[s, there, :] = sums[s * lines : (s + 1) * lines, t * 128 : (t + 1) * 128]

    load_wout.wait()
    wout[...] = wout_raw[...].T
    load_win.wait()
    load_lens.wait()
    pending = None
    for i in range(chunks):
        part = pl.ds(i * rows, rows)
        wait(2 * i)
        start(2 * i + 3)
        gp = jnp.dot(grad_buf[part, :], wout[...], preferred_element_type=F32)
        if i == 0:
            win[...] = win_raw[...].T
        else:
            add_up(*pending)
        left = gp.T.astype(BF16)
        if i < chunks - 1:
            wait(2 * i + 1)
            start(2 * i + 4)
            xp = jnp.dot(act_buf[part, :], win[...], preferred_element_type=F32)
        else:
            pieces = []
            for h, load in enumerate(loads[2 * i + 1]):
                load.wait()
                piece = pl.ds(i * rows + h * (rows // 2), rows // 2)
                pieces.append(jnp.dot(act_buf[piece, :], win[...], preferred_element_type=F32))
            xp = jnp.concatenate(pieces, axis=0)
        pending = (i, left, xp)
    add_up(*pending)
    core = lax.rem(grp, 2)
    for x in range(groups // 2):
        send[x] = store[2 * x + 1 - core]
        keep[x] = store[2 * x + core]


def fold_kernel(keep, came, *rest):
    send, kept = rest[-2:]
    x = lax.axis_index("grp") // 2
    send[...] = (keep[1 - x] + came[1 - x]).astype(BF16)
    kept[...] = keep[x] + came[x]


def combine_kernel(dims, kept, came, *rest):
    half, lines, width = dims
    out, squares, grads = rest[-3:]
    grads[...] = kept[...] + came[...].astype(F32)
    low = lax.broadcasted_iota(jnp.int32, (half, 128), 1) < width
    sums, columns = None, []
    for e in range(0, lines, 2):
        first = grads[pl.ds(e, half, stride=lines), :]
        second = grads[pl.ds(e + 1, half, stride=lines), :]
        line = jnp.concatenate(
            [
                jnp.where(low, first, pltpu.roll(second, width, 1)),
                jnp.where(low, pltpu.roll(first, width, 1), second),
            ],
            axis=0,
        )
        columns.append(line.astype(BF16))
        sums = line * line if sums is None else sums + line * line
    squares[...] = sums
    out[...] = jnp.concatenate(columns, axis=1)


def join_kernel(count, *refs):
    out = refs[-1]
    nq = refs[-2].shape[0]
    for n, ref in enumerate(refs[-1 - count : -1]):
        out[n * nq : (n + 1) * nq, :] = ref[...]


def near_kernel(dims, left, *refs):
    blk = lax.axis_index("blk")
    place = refs[-1]
    for flip, piece in zip(dims, refs[:-1]):
        place[jnp.bitwise_xor(blk, flip)] = lax.dot_general(
            left[...], piece[...], BY_ROWS, preferred_element_type=F32
        )


def scores_kernel(dims, left, squares, near, late, passed, *rest):
    blks, groups = dims
    outs = rest[:groups]
    place, result = rest[groups:]
    rows = left[...]
    blk = lax.axis_index("blk")
    nq = near.shape[2]
    place[...] = near[...]
    place[jnp.bitwise_xor(blk, 2)] = lax.dot_general(
        rows, late[...], BY_ROWS, preferred_element_type=F32
    )
    for n in range(blks // 2 - 2):
        place[jnp.bitwise_xor(blk, blks - 1 - 2 * n)] = lax.dot_general(
            rows, passed[n * nq : (n + 1) * nq, :], BY_ROWS, preferred_element_type=F32
        )
    scores = jnp.concatenate([place[b] for b in range(blks)], axis=1)
    width = blks * nq
    half = scores.shape[0] // 2
    owned = half // groups
    for g in range(groups):
        for h in range(2):
            here = slice(h * half + g * owned, h * half + (g + 1) * owned)
            there = slice(h * owned, (h + 1) * owned)
            result[g, there, :width] = scores[here]
            result[g, there, width:] = squares[here, :]
    grp = lax.axis_index("grp")
    for k in range(groups):
        outs[k][...] = result[jnp.bitwise_xor(grp, k)]


def finish_kernel(pdim, *refs):
    out = refs[-1]
    total = refs[0][...]
    for ref in refs[1:-1]:
        total = total + ref[...]
    width = out.shape[1]
    mean = jnp.sum(total[:, width:], axis=1, keepdims=True) / pdim
    out[...] = total[:, :width] * lax.rsqrt(mean + EPS)


def small(kernel, out_shape, operands, scratch_shapes=(), name=None):
    one = not isinstance(out_shape, list)
    return pl.pallas_call(
        kernel,
        out_shape=out_shape,
        in_specs=[VMEM] * len(operands),
        out_specs=VMEM if one else [VMEM] * len(out_shape),
        scratch_shapes=list(scratch_shapes),
        compiler_params=pltpu.CompilerParams(vmem_limit_bytes=16 * 2**20),
        name=name,
    )(*operands)


def on_device(blks, groups, acts, out_grads, proj_in, proj_out, lengths, queries):
    _, cands, tokens, depth = acts.shape
    width = proj_in.shape[2]
    far = blks // 2
    pdim = width * width
    lines = width // groups
    nq = queries.shape[0]
    total_q = nq * blks
    owned = cands // groups
    slice_width = pdim // groups
    shape = jax.ShapeDtypeStruct

    def grp_swap(x, k):
        return lax.ppermute(x, "grp", [(g, g ^ k) for g in range(groups)])

    def blk_swap(x, k):
        return lax.ppermute(x, "blk", [(b, b ^ k) for b in range(blks)])

    cut = lax.dynamic_slice(queries, (0, lax.axis_index("grp") * slice_width), (nq, slice_width))
    cut, lens = lax.optimization_barrier((cut, jnp.minimum(lengths, tokens * groups)))
    pieces = [cut, blk_swap(cut, 1), blk_swap(cut, 3)]
    distant = [blk_swap(cut, 2 * k) for k in range(2, far)]

    rows = cands * tokens
    piece = (cands // 2 * lines, 128)
    send, keep = pl.pallas_call(
        functools.partial(grads_kernel, (cands, tokens, width, groups)),
        out_shape=[shape((groups // 2,) + piece, F32)] * 2,
        in_specs=[ANY] * 5,
        out_specs=[VMEM] * 2,
        scratch_shapes=[
            pltpu.VMEM((rows, depth), BF16),
            pltpu.VMEM((rows, depth), BF16),
            pltpu.VMEM((width, depth), BF16),
            pltpu.VMEM((width, depth), BF16),
            pltpu.VMEM((depth, width), BF16),
            pltpu.VMEM((depth, width), BF16),
            pltpu.SMEM((cands,), jnp.int32),
            pltpu.VMEM((groups,) + piece, F32),
            pltpu.SemaphoreType.DMA((2, cands // 2)),
            pltpu.SemaphoreType.DMA((3,)),
        ],
        compiler_params=pltpu.CompilerParams(vmem_limit_bytes=GRANT * 2**10),
        cost_estimate=pl.CostEstimate(
            flops=16 * rows * depth * width, bytes_accessed=4 * rows * depth, transcendentals=0
        ),
        name="grads",
    )(
        lens,
        acts.reshape(rows, depth),
        out_grads.reshape(rows, depth),
        proj_in[0].T,
        proj_out[0].T,
    )
    joined = small(
        functools.partial(join_kernel, far - 2),
        shape(((far - 2) * nq, slice_width), BF16),
        (*pieces[1:], keep, *distant[::-1]),
        name="join",
    )
    late, joined = lax.optimization_barrier((cut, joined))
    late = blk_swap(late, 2)
    send, kept = small(
        fold_kernel,
        [shape(piece, BF16), shape(piece, F32)],
        (keep, grp_swap(send, 1), joined),
        name="fold",
    )
    passed = blk_swap(joined, 1)
    own, squares = small(
        functools.partial(combine_kernel, (cands // 2, lines, width)),
        [shape((cands, slice_width), BF16), shape((cands, 128), F32)],
        (kept, grp_swap(send, 2)),
        [pltpu.VMEM(piece, F32)],
        name="combine",
    )
    near = small(
        functools.partial(near_kernel, [0, 1, 3] + [2 * k for k in range(2, far)]),
        shape((blks, cands, nq), F32),
        (own, *pieces, *distant),
        name="near",
    )
    line = (owned, total_q + 128)
    sums = small(
        functools.partial(scores_kernel, (blks, groups)),
        [shape(line, F32)] * groups,
        (own, squares, near, late, passed),
        [pltpu.VMEM((blks, cands, nq), F32), pltpu.VMEM((groups,) + line, F32)],
        name="scores",
    )
    return small(
        functools.partial(finish_kernel, pdim),
        shape((owned, total_q), F32),
        (sums[0], *[grp_swap(sums[k], k) for k in range(groups - 1, 0, -1)]),
        name="finish",
    )


def solution(mesh):
    in_specs = (
        P(None, "blk", "grp", None),
        P(None, "blk", "grp", None),
        P(),
        P(),
        P("blk"),
        P("blk", None),
    )
    return jax.shard_map(
        functools.partial(on_device, mesh.shape["blk"], mesh.shape["grp"]),
        mesh=mesh,
        in_specs=in_specs,
        out_specs=P(("blk", "grp"), None),
        check_vma=False,
    )
```
